32 devices in a mesh: seq: 2 (over x), batch: 16 (over z, y, core).
Axes of the slice: x: 2, y: 2, z: 4, core: 2. Of those that a mesh axis runs over, the one named last changes fastest.
Arguments:
- inputs: bfloat16 [16, 1024, 768], P('batch', 'seq'), may hold values from -6 to 6
- cotangent: bfloat16 [16, 1024, 768], P('batch', 'seq'), may hold values from -6 to 6
- cond_mask: int32 [16], P('batch'), may hold values 0 or 1
- timestep: int32 [16], P('batch'), may hold values from 0 to 999
- embed_table: float32 [1000, 768], replicated, may hold values from -6 to 6
- mix_weight: bfloat16 [768, 2304], replicated, may hold values from -0.21875 to 0.21875
- project_weight: bfloat16 [768, 768], replicated, may hold values from -3 to 3
- up_weight: bfloat16 [768, 3072], replicated, may hold values from -0.21875 to 0.21875
- down_weight: bfloat16 [3072, 768], replicated, may hold values from -0.109375 to 0.109375
- cond_weight: bfloat16 [768, 4608], replicated, may hold values from -0.21875 to 0.21875
- cond_bias: float32 [4608], replicated, may hold values from -3 to 3
Outputs:
- layer_output: bfloat16 [16, 1024, 768], P('batch', 'seq')
- input_grad: float32 [16, 1024, 768], P('batch', 'seq')
- grad_mix: float32 [768, 2304], P('batch')
- grad_project: float32 [768, 768], P('batch')
- grad_up: float32 [768, 3072], P('batch')
- grad_down: float32 [3072, 768], P('batch')
- grad_cond: float32 [768, 4608], P('batch')
- grad_bias: float32 [4608], P('batch')
The draws below stay inside these ranges and needn't reach their ends.
All inputs are finite; a program needn't handle non-finite values. No bound on the sum of `cond_mask` on one device may be relied on, other than what follows from the above.
Results may differ from the reference program's by a relative error of at most 0.01.
The reference program's roundings to bfloat16 on the way (of `a_in` and `mixed`) count: a program that leaves them out, or rounds other values in their place, can miss the bound.
Values may be sent and summed in bfloat16 or wider, within the bound.
A program may use at most 256 MiB of HBM per device.

```python
import jax
import jax.numpy as jnp
from jax import lax

D = 768
HEAD = 64
FF = 3072
TSTEPS = 1000
LENGTH = 1024
BATCH = 16


def set_ends(entries, stream_key, low, top_value):
    longest = entries.shape.index(max(entries.shape))
    spots = []
    for shift in (0, 1):
        where = [jax.random.randint(jax.random.fold_in(stream_key, axis), (), 0, length) for axis, length in enumerate(entries.shape)]
        where[longest] = (where[longest] + shift) % entries.shape[longest]
        spots.append(tuple(where))
    return entries.at[spots[0]].set(low).at[spots[1]].set(top_value)


def block_levels(rng, dims, pieces, low, largest):
    gain, own = 1.0, jax.random.fold_in(rng, 6)
    for position, parts in pieces:
        steps = jnp.exp(jax.random.uniform(jax.random.fold_in(own, position), (parts,), jnp.float32, low / len(pieces), largest / len(pieces)))
        gain = gain * jnp.repeat(steps, dims[position] // parts).reshape([-1 if axis == position else 1 for axis in range(len(dims))])
    return gain


def noise(key, extent, spread, limit, shards=(), kind=jnp.bfloat16):
    array = jax.random.normal(key, extent, jnp.float32) * spread
    if len(shards) > 0:
        array = block_levels(key, extent, shards, -0.22, 0.18) * array
    return jnp.clip(array, min=-limit, max=limit).astype(kind)


def setup_inputs(seed: int = 0) -> dict:
    arg_keys = jax.random.split(jax.random.key(seed), 12)
    inputs = noise(arg_keys[0], (BATCH, LENGTH, D), 1.0, 6.0, ((0, 16), (1, 2)))
    cotangent = noise(arg_keys[1], (BATCH, LENGTH, D), 1.0, 6.0, ((0, 16), (1, 2)))
    cond_mask = set_ends((jax.random.randint(arg_keys[2], (BATCH,), 0, 2) < 1).astype(jnp.int32), jax.random.fold_in(arg_keys[2], 1), 0, 1)
    timestep = set_ends(jax.random.randint(arg_keys[3], (BATCH,), 0, TSTEPS), jax.random.fold_in(arg_keys[3], 1), 0, TSTEPS - 1).astype(jnp.int32)
    embed_table = noise(arg_keys[4], (TSTEPS, D), 1.0, 6.0, (), jnp.float32)
    mix_weight = noise(arg_keys[5], (D, 3 * D), D ** -0.5, 0.21875)
    project_weight = noise(arg_keys[6], (D, D), (max(4, D // 256)) ** -0.5, 3.0)
    up_weight = noise(arg_keys[7], (D, FF), D ** -0.5, 0.21875)
    down_weight = noise(arg_keys[8], (FF, D), FF ** -0.5, 0.109375)
    cond_weight = noise(arg_keys[9], (D, 6 * D), D ** -0.5, 0.21875)
    cond_bias = noise(arg_keys[10], (6 * D,), 0.5, 3.0, (), jnp.float32)
    return dict(inputs=inputs, cotangent=cotangent, cond_mask=cond_mask, timestep=timestep, embed_table=embed_table, mix_weight=mix_weight, project_weight=project_weight, up_weight=up_weight, down_weight=down_weight, cond_weight=cond_weight, cond_bias=cond_bias)


@jax.custom_vjp
def low(v):
    return lax.optimization_barrier(v.astype(jnp.bfloat16)).astype(jnp.float32)

@jax.custom_vjp
def low_back(v):
    return v

def low_keep(v):
    return (low(v), None)

def low_pass(kept, grad):
    return (grad,)

def back_keep(v):
    return (v, None)

def back_low(kept, grad):
    return (low(grad),)
low.defvjp(low_keep, low_pass)
low_back.defvjp(back_keep, back_low)
eps_norm = 1e-06
theta_base = 10000.0
highest = lax.Precision.HIGHEST

def normalize(values):
    row_mean = lax.optimization_barrier(jnp.mean(values, axis=-1, keepdims=True))
    centered = values - row_mean
    row_var = lax.optimization_barrier(jnp.mean(centered * centered, axis=-1, keepdims=True))
    return centered * lax.rsqrt(row_var + eps_norm)

def rotary_tables(count, offset, head_size):
    half_size = head_size // 2
    freqs = theta_base ** (-jnp.arange(half_size, dtype=jnp.float32) * 2.0 / head_size)
    places = (offset + jnp.arange(count, dtype=jnp.int32)).astype(jnp.float32)
    angles = places[:, None] * freqs[None, :]
    return (jnp.cos(angles)[:, None, :], jnp.sin(angles)[:, None, :])

def rotate(values, cosine_table, sine_table):
    half_size = values.shape[-1] // 2
    first_half = values[..., :half_size]
    second = values[..., half_size:]
    return jnp.concatenate([first_half * cosine_table - second * sine_table, second * cosine_table + first_half * sine_table], axis=-1)

def block(xin, embedding, params, cosine_table, sine_table):
    mix_weight, project_weight, up_weight, down_weight, cond_weight, cond_bias = params
    length_here = xin.shape[0]
    model_width = xin.shape[1]
    head_count = model_width // HEAD
    cond_code = low(jax.nn.silu(embedding))
    modulation = jnp.dot(cond_code, cond_weight, precision=highest) + cond_bias
    shift_mix, scale_mix, gate_mix, shift_feed, scale_feed, gate_feed = [modulation[slot_index * model_width:(slot_index + 1) * model_width] for slot_index in range(6)]
    a_in = low(normalize(xin) * (1.0 + scale_mix) + shift_mix)
    projected = low_back(jnp.dot(a_in, mix_weight, precision=highest)).reshape(length_here, 3, head_count, HEAD)
    query = low(rotate(projected[:, 0], cosine_table, sine_table))
    key_part = low(rotate(projected[:, 1], cosine_table, sine_table))
    value_part = low(projected[:, 2])
    scores = low_back(jnp.einsum('qhe,khe->hqk', query, key_part, precision=highest) * HEAD ** (-0.5))
    probs = low(jax.nn.softmax(scores, axis=-1))
    mixed = low_back(low(jnp.einsum('hqk,khe->qhe', probs, value_part, precision=highest)))
    branch_mix = low_back(jnp.dot(mixed.reshape(length_here, model_width), project_weight, precision=highest))
    middle = xin + gate_mix * branch_mix
    b_in = low(normalize(middle) * (1.0 + scale_feed) + shift_feed)
    hidden = low(jax.nn.gelu(low_back(jnp.dot(b_in, up_weight, precision=highest))))
    branch_feed = low_back(jnp.dot(hidden, down_weight, precision=highest))
    return middle + gate_feed * branch_feed

def reference(inputs, cotangent, cond_mask, timestep, embed_table, mix_weight, project_weight, up_weight, down_weight, cond_weight, cond_bias):
    params = tuple((weight.astype(jnp.float32) for weight in (mix_weight, project_weight, up_weight, down_weight, cond_weight, cond_bias)))
    cosine_table, sine_table = rotary_tables(LENGTH, 0, HEAD)

    def per_sequence(totals, sequence_item):
        seq_input, seq_cot, cond_flag, time_step = sequence_item
        embedding = embed_table[time_step]
        inputs_f32 = seq_input.astype(jnp.float32)
        first_pass = block(inputs_f32, embedding, params, cosine_table, sine_table)
        xin = inputs_f32 + cond_flag.astype(jnp.float32) * first_pass
        output, pull_back = jax.vjp(lambda values, weights: block(values, embedding, weights, cosine_table, sine_table), xin, params)
        grad_in, grad_params = pull_back(seq_cot.astype(jnp.float32))
        totals = tuple((total + grad for total, grad in zip(totals, grad_params)))
        return (totals, (output.astype(jnp.bfloat16), grad_in))
    start_totals = tuple((jnp.zeros_like(weight) for weight in params))
    totals, (outputs, grads) = lax.scan(per_sequence, start_totals, (inputs, cotangent, cond_mask, timestep))
    return (outputs, grads, totals[0], totals[1], totals[2], totals[3], totals[4], totals[5])
```

```python
import functools
import math

import jax
import jax.numpy as jnp
import numpy as np
from jax import lax
from jax.experimental import pallas as pl
from jax.experimental.pallas import tpu as pltpu
from jax.sharding import PartitionSpec as P

HEAD = 64
PAIR = 2 * HEAD
ITER = 2 * PAIR
EPS = 1e-06
THETA = 10000.0
LOG2E = 1.4426950408889634
SCALE = HEAD ** (-0.5)
EXP_SCALE = SCALE * LOG2E
GELU_A = math.sqrt(2.0 / math.pi)
GELU_B = 0.044715
BF = jnp.bfloat16
F32 = jnp.float32
MESH = pl.DeviceIdType.MESH
ROWS_LN = 128


def dot(left, right, left_dim=1, right_dim=0):
    return lax.dot_general(
        left, right, (((left_dim,), (right_dim,)), ((), ())), preferred_element_type=F32
    )


def lanes(shape):
    return lax.broadcasted_iota(jnp.int32, shape, len(shape) - 1)


def one_head(values, head):
    return jnp.where((lanes(values.shape) // HEAD) == head, values, jnp.zeros_like(values))


def bit_of(value, bit):
    return lax.rem(value // bit, 2)


def flip(value, bit):
    return value + bit - 2 * bit * bit_of(value, bit)


def aligned(value, unit):
    return pl.multiple_of(value, unit)


def rotary_constants(length):
    half_size = HEAD // 2
    freqs = THETA ** (-np.arange(half_size, dtype=np.float64) * 2.0 / HEAD)
    angles = np.arange(length, dtype=np.float64)[:, None] * freqs[None, :]
    cosine, sine = np.cos(angles), np.sin(angles)
    cosine = np.concatenate([cosine] * 4, axis=1).astype(np.float32)
    sine = np.concatenate([-sine, sine] * 2, axis=1).astype(np.float32)
    return cosine, sine


def swap_halves(values):
    first = lax.rem(lanes(values.shape), HEAD) < HEAD // 2
    return jnp.where(
        first, pltpu.roll(values, PAIR - HEAD // 2, 1), pltpu.roll(values, HEAD // 2, 1)
    )


def normalize(values):
    row_mean = jnp.mean(values, axis=-1, keepdims=True)
    centered = values - row_mean
    row_var = jnp.mean(centered * centered, axis=-1, keepdims=True)
    inverse = lax.rsqrt(row_var + EPS)
    return centered * inverse, inverse


def norm_back(grad_normed, normed, inverse):
    grad_mean = jnp.mean(grad_normed, axis=-1, keepdims=True)
    cross_mean = jnp.mean(grad_normed * normed, axis=-1, keepdims=True)
    return inverse * (grad_normed - grad_mean - normed * cross_mean)


def col_sum(values):
    return jnp.sum(values, axis=0, keepdims=True)


def bits_of(count):
    return [1 << k for k in range(count.bit_length() - 1)]


def wait_bytes(ref, sem):
    pltpu.make_async_copy(ref, ref, sem).wait()


class Job:
    def __init__(self, grad, out, first, width, seq_early, sizes):
        self.grad, self.out, self.first, self.width = grad, out, first, width
        self.seq_count, self.batch_count = sizes
        self.row_block = grad.shape[0] // self.batch_count
        self.fold = 1
        while self.row_block * self.fold % 16:
            self.fold *= 2
        self.unit = self.row_block * self.fold
        self.units = self.batch_count // self.fold
        halvings = [("batch", bit) for bit in bits_of(self.units)]
        if seq_early and self.fold == 1 and (width // self.seq_count) % PAIR == 0:
            self.stages = (
                halvings[:1]
                + [("cut", bit) for bit in bits_of(self.seq_count)]
                + halvings[1:]
                + [("gather", bit) for bit in bits_of(self.seq_count)[::-1]]
            )
        else:
            self.stages = (
                halvings
                + [("add", bit) for bit in bits_of(self.seq_count)]
                + [("fold", bit) for bit in bits_of(self.fold)]
            )

    def landing_shapes(self):
        count, width, shapes = self.units, self.width, []
        for kind, _ in self.stages:
            if kind == "batch":
                count //= 2
            elif kind == "cut":
                width //= 2
            shapes.append((count * self.unit, width))
            if kind == "gather":
                width *= 2
        return shapes


def job_list(grads, outs, sizes):
    grad_down, grad_up, grad_project, grad_mix = grads
    out_down, out_up, out_project, out_mix = outs
    model_width, hidden_width = grad_up.shape
    jobs = {}
    jobs["down_y"] = Job(grad_down, out_down, 0, ITER, False, sizes)
    jobs["down_x"] = Job(grad_down, out_down, ITER, model_width - ITER, True, sizes)
    jobs["up_y"] = Job(grad_up, out_up, 0, hidden_width // 2, False, sizes)
    jobs["up_x"] = Job(grad_up, out_up, hidden_width // 2, hidden_width // 2, True, sizes)
    jobs["project"] = Job(grad_project, out_project, 0, model_width, False, sizes)
    for i in range(model_width // ITER):
        jobs[f"mix{i}_x"] = Job(grad_mix, out_mix, i * 3 * ITER, 2 * ITER, True, sizes)
        jobs[f"mix{i}_y"] = Job(grad_mix, out_mix, i * 3 * ITER + 2 * ITER, ITER, False, sizes)
    return jobs


def step_kernel(
    sizes,
    seqs_here,
    pos_here,
    inputs_hbm,
    cot_hbm,
    codes_ref,
    bias_ref,
    cos_hbm,
    sin_hbm,
    mix_hbm,
    project_hbm,
    up_hbm,
    down_hbm,
    cond_hbm,
    layer_hbm,
    igrad_hbm,
    out_mix,
    out_project,
    out_up,
    out_down,
    out_all,
    mix,
    project,
    up,
    down,
    cos,
    sin,
    x16,
    cot,
    x,
    x1,
    a_in,
    q,
    kv,
    kv_other,
    mixed,
    branch,
    b_in,
    slope,
    hidden,
    gbf,
    gx,
    dout,
    dkv,
    lse,
    mod,
    codes_other,
    gsum,
    gsum_other,
    landings,
    load_sem,
    share_sem,
    share_recv,
    kv_sem,
    kv_recv,
    dkv_sem,
    dkv_recv,
    small_sem,
    small_recv,
    job_sem,
    job_recv,
):
    seq_count, batch_count = sizes
    rows, width = x.shape
    hidden_width = up.shape[1]
    pairs = width // PAIR
    iters = width // ITER
    block = 3 * ITER
    s = lax.axis_index("seq")
    b = lax.axis_index("batch")
    core = lax.rem(b, 2)
    core_peer = (s, flip(b, 1))

    barrier = pltpu.get_barrier_semaphore()
    peers = [(s, flip(b, bit)) for bit in bits_of(batch_count)]
    peers += [(flip(s, bit), b) for bit in bits_of(seq_count)]
    for peer in peers:
        pl.semaphore_signal(barrier, inc=1, device_id=peer, device_id_type=MESH)

    def share_peer(j):
        return core * seqs_here + j, b - core + s // seqs_here

    def is_self(j):
        ps, pb = share_peer(j)
        return jnp.logical_and(ps == s, pb == b)

    for j in range(seqs_here):

        @pl.when(jnp.logical_not(is_self(j)))
        def _():
            pl.semaphore_signal(barrier, inc=1, device_id=share_peer(j), device_id_type=MESH)

    own = jnp.where(s // seqs_here == core, 1, 0)

    cond_up = pltpu.make_async_copy(cond_hbm.at[:, pl.ds(0, hidden_width)], up, load_sem.at[0])
    cond_up.start()
    rest = cond_hbm.shape[1] - hidden_width
    cond_down = []
    for i in range(rest // width):
        cond_down.append(
            pltpu.make_async_copy(
                cond_hbm.at[:, pl.ds(hidden_width + i * width, width)],
                down.at[pl.ds(i * width, width), :],
                load_sem.at[1 + i],
            )
        )
        cond_down[-1].start()
    mix_loads = []
    for i in range(iters):
        for part in range(3):
            mix_loads.append(
                pltpu.make_async_copy(
                    mix_hbm.at[:, pl.ds(part * width + i * ITER, ITER)],
                    mix.at[:, pl.ds(i * block + part * ITER, ITER)],
                    load_sem.at[8],
                )
            )
            mix_loads[-1].start()
    row0 = core * rows
    load_cos = pltpu.make_async_copy(
        cos_hbm.at[pl.ds(aligned(row0, 128), rows), :], cos, load_sem.at[5]
    )
    load_sin = pltpu.make_async_copy(
        sin_hbm.at[pl.ds(aligned(row0, 128), rows), :], sin, load_sem.at[6]
    )
    load_project = pltpu.make_async_copy(project_hbm, project, load_sem.at[7])
    load_cos.start()
    load_sin.start()
    load_project.start()

    pl.semaphore_wait(barrier, len(peers) + seqs_here - own)

    def share_copy(source, target, j, k):
        return pltpu.make_async_remote_copy(
            src_ref=source,
            dst_ref=target,
            send_sem=share_sem.at[k],
            recv_sem=share_recv.at[k],
            device_id=share_peer(j),
            device_id_type=MESH,
        )

    slot = lax.rem(s, seqs_here)

    def share_start(source, target, k):
        for j in range(seqs_here):

            @pl.when(is_self(j))
            def _():
                pltpu.make_async_copy(source(j), target(slot), share_recv.at[k]).start()

            @pl.when(jnp.logical_not(is_self(j)))
            def _():
                share_copy(source(j), target(slot), j, k).start()

    def share_sent(source, target, k):
        for j in range(seqs_here):

            @pl.when(jnp.logical_not(is_self(j)))
            def _():
                share_copy(source(j), target(slot), j, k).wait_send()

    def rows_of(ref):
        return lambda j: ref.at[pl.ds(aligned(j * pos_here, 16), pos_here), :]

    def seq_of(ref):
        return lambda j: ref.at[j]

    def to_core(source, target, sems, recvs, k):
        return pltpu.make_async_remote_copy(
            src_ref=source,
            dst_ref=target,
            send_sem=sems.at[k],
            recv_sem=recvs.at[k],
            device_id=core_peer,
            device_id_type=MESH,
        )

    code_copy = to_core(codes_ref, codes_other, small_sem, small_recv, 0)
    code_copy.start()
    share_start(seq_of(inputs_hbm), rows_of(x16), 0)
    share_start(seq_of(cot_hbm), rows_of(cot), 1)

    code_copy.wait()
    own_f = own.astype(F32)
    code_rows = codes_ref[...] * own_f + codes_other[...] * (1.0 - own_f)
    row_ids = lax.broadcasted_iota(jnp.int32, code_rows.shape, 0)
    half_rows = code_rows.shape[0] // 2
    code = col_sum(jnp.where(row_ids == slot, code_rows, 0.0))
    flag = col_sum(jnp.where(row_ids == slot + half_rows, code_rows, 0.0))
    code_lhs = jnp.broadcast_to(code, (8, width)).astype(BF)
    cond_up.wait()
    for piece in range(hidden_width // width):
        at = slice(piece * width, (piece + 1) * width)
        mod[:, at] = dot(code_lhs, up[:, at]) + bias_ref[:, at]
    load_up = pltpu.make_async_copy(up_hbm, up, load_sem.at[0])
    load_up.start()
    for i in range(rest // width):
        cond_down[i].wait()
        at = slice(hidden_width + i * width, hidden_width + (i + 1) * width)
        mod[:, at] = dot(code_lhs, down[i * width : (i + 1) * width, :]) + bias_ref[:, at]
    load_down = pltpu.make_async_copy(down_hbm, down, load_sem.at[1])
    load_down.start()

    def piece_of(index, start=0, size=None):
        size = width if size is None else size
        return mod[0:1, pl.ds(index * width + start, size)]

    SHIFT_MIX, SCALE_MIX, GATE_MIX, SHIFT_FEED, SCALE_FEED, GATE_FEED = range(6)

    def norm_rows(source, target, shift_index, scale_index):
        def body(i, _):
            at = pl.ds(aligned(i * ROWS_LN, ROWS_LN), ROWS_LN)
            normed, _ = normalize(source[at, :].astype(F32))
            target[at, :] = (
                normed * (1.0 + piece_of(scale_index)) + piece_of(shift_index)
            ).astype(BF)
            return 0

        lax.fori_loop(0, rows // ROWS_LN, body, 0)

    def rotate(values, sign):
        parts = []
        for p in range(values.shape[1] // PAIR):
            part = values[:, p * PAIR : (p + 1) * PAIR]
            parts.append(part * cos[...] + sign * (swap_halves(part) * sin[...]))
        return jnp.concatenate(parts, axis=1)

    def project_part(part, target, base):
        def body(i, _):
            made = dot(a_in[...], mix[:, pl.ds(aligned(i * block + part * ITER, ITER), ITER)])
            if part < 2:
                made = rotate(made, 1.0)
            target[:, pl.ds(aligned(base + i * ITER, ITER), ITER)] = made.astype(BF)
            return 0

        lax.fori_loop(0, iters, body, 0)

    def kv_copy(which, part):
        at = pl.ds(part * width, width)
        return to_core(kv.at[:, at], kv_other.at[which, :, at], kv_sem, kv_recv, 2 * which + part)

    def attend(which):
        group = pairs // 2

        def body(i, _):
            for inner in range(group):
                pair = i * group + inner
                at = pl.ds(aligned(pair * PAIR, PAIR), PAIR)
                at_v = pl.ds(aligned(width + pair * PAIR, PAIR), PAIR)
                query = q[:, at]
                key = jnp.concatenate([kv[:, at], kv_other[which, :, at]], axis=0)
                value = jnp.concatenate([kv[:, at_v], kv_other[which, :, at_v]], axis=0)
                outs = []
                for head in range(2):
                    scores = dot(one_head(query, head), key, 1, 1)
                    top = jnp.max(scores, axis=1, keepdims=True)
                    weights = jnp.exp2((scores - top) * EXP_SCALE)
                    ones = jnp.where(
                        (lanes(value.shape) // HEAD) == head, value, jnp.ones_like(value)
                    )
                    made = dot(weights.astype(BF), ones)
                    total = made[:, HEAD * (1 - head) : HEAD * (1 - head) + 1]
                    outs.append(made * (1.0 / total))
                    if which == 1:
                        level = top * EXP_SCALE + jnp.log2(total)
                        lse[...] = jnp.where(
                            lanes(lse.shape) == 2 * pair + head, level, lse[...]
                        )
                mixed[:, at] = jnp.where(
                    lanes(outs[0].shape) < HEAD, outs[0], outs[1]
                ).astype(BF)
            return 0

        lax.fori_loop(0, 2, body, 0)

    def forward(which):
        if which == 0:
            wait_bytes(x16, share_recv.at[0])
        norm_rows(x16 if which == 0 else x, a_in, SHIFT_MIX, SCALE_MIX)
        if which == 0:
            for load in mix_loads:
                load.wait()
            load_cos.wait()
            load_sin.wait()
        project_part(1, kv, 0)
        key_copy = kv_copy(which, 0)
        key_copy.start()
        project_part(2, kv, width)
        value_copy = kv_copy(which, 1)
        value_copy.start()
        project_part(0, q, 0)
        key_copy.wait()
        value_copy.wait()
        attend(which)
        if which == 0:
            load_project.wait()

        def mix_out(i, _):
            at = pl.ds(aligned(i * ITER, ITER), ITER)
            made = dot(mixed[...], project[:, at])
            if which == 1:
                branch[:, at] = made.astype(BF)
            base = x16[:, at].astype(F32) if which == 0 else x[:, at]
            gate = mod[0:1, pl.ds(aligned(GATE_MIX * width + i * ITER, ITER), ITER)]
            x1[:, at] = base + gate * made
            return 0

        lax.fori_loop(0, iters, mix_out, 0)
        norm_rows(x1, b_in, SHIFT_FEED, SCALE_FEED)
        if which == 0:
            load_up.wait()
        step = 2 * ITER

        def feed_up(i, _):
            at = pl.ds(aligned(i * step, step), step)
            pre = dot(b_in[...], up[:, at])
            square = pre * pre
            inner = jnp.tanh(pre * (GELU_A + (GELU_A * GELU_B) * square))
            left = 0.5 * (1.0 + inner)
            hidden[:, at] = (pre * left).astype(BF)
            if which == 1:
                bend = GELU_A + (3.0 * GELU_A * GELU_B) * square
                slope[:, at] = (left + (0.5 * pre) * (1.0 - inner * inner) * bend).astype(BF)
            return 0

        lax.fori_loop(0, hidden_width // step, feed_up, 0)
        if which == 0:
            load_down.wait()

        def feed_down(i, _):
            at = pl.ds(aligned(i * ITER, ITER), ITER)
            made = dot(hidden[...], down[:, at])
            gate = mod[0:1, pl.ds(aligned(GATE_FEED * width + i * ITER, ITER), ITER)]
            result = x1[:, at] + gate * made
            if which == 0:
                x[:, at] = x16[:, at].astype(F32) + flag[:, 0:1] * result
            else:
                x16[:, at] = result.astype(BF)
                grad = cot[:, at].astype(F32)
                mod[1:2, pl.ds(aligned(GATE_FEED * width + i * ITER, ITER), ITER)] = col_sum(
                    grad * made
                )
                gbf[:, at] = (gate * grad).astype(BF)
            return 0

        lax.fori_loop(0, iters, feed_down, 0)

    forward(0)
    share_sent(seq_of(inputs_hbm), rows_of(x16), 0)
    wait_bytes(cot, share_recv.at[1])
    share_sent(seq_of(cot_hbm), rows_of(cot), 1)
    forward(1)
    share_start(rows_of(x16), seq_of(layer_hbm), 2)

    jobs = job_list((down, up, project, mix), (out_down, out_up, out_project, out_mix), sizes)
    landing_at, sem_at = 0, 0
    for job in jobs.values():
        job.landing = landings[landing_at : landing_at + len(job.stages)]
        job.sem_base = sem_at
        landing_at += len(job.stages)
        sem_at += len(job.stages)

    def job_view(job, stage):
        stride, start, wide = 1, job.first, job.width
        for kind, bit in job.stages[:stage]:
            if kind == "batch":
                stride = 2 * bit
            elif kind == "cut":
                wide //= 2
                start = start + bit_of(s, bit) * wide
        return stride, start, wide

    def gather_view(job, stage):
        start, wide = job.first, job.width
        done = [bit for kind, bit in job.stages[:stage] if kind == "gather"]
        for kind, bit in job.stages:
            if kind == "cut" and bit not in done:
                wide //= 2
                start = start + bit_of(s, bit) * wide
        return start, wide

    def job_copies(job, stage):
        kind, bit = job.stages[stage]
        land = job.landing[stage]
        height, fold = job.unit, job.fold
        me = b // fold
        k = job.sem_base + stage
        copies = []

        def add(row, start, wide, target, peer):
            source = job.grad.at[
                pl.ds(aligned(row * height, height), height), pl.ds(aligned(start, PAIR), wide)
            ]
            copies.append(
                pltpu.make_async_remote_copy(
                    src_ref=source,
                    dst_ref=target,
                    send_sem=job_sem.at[k],
                    recv_sem=job_recv.at[k],
                    device_id=peer,
                    device_id_type=MESH,
                )
            )

        stride, start, wide = job_view(job, stage)
        if kind == "batch":
            for t in range(job.units // (2 * bit)):
                row = lax.rem(me, bit) + (1 - bit_of(me, bit)) * bit + t * 2 * bit
                there = land.at[pl.ds(t * height, height), :]
                add(row, start, wide, there, (s, flip(b, bit * fold)))
        elif kind == "cut":
            half = wide // 2
            for t in range(job.units // stride):
                row = lax.rem(me, stride) + t * stride
                add(
                    row,
                    start + (1 - bit_of(s, bit)) * half,
                    half,
                    land.at[pl.ds(t * height, height), :],
                    (flip(s, bit), b),
                )
        elif kind == "add":
            add(me, start, wide, land, (flip(s, bit), b))
        elif kind == "fold":
            add(me, start, wide, land, (s, flip(b, bit)))
        else:
            start, wide = gather_view(job, stage)
            add(me, start, wide, land, (flip(s, bit), b))
        return copies

    def job_start(name, stage):
        for copy in job_copies(jobs[name], stage):
            copy.start()

    def job_finish(name, stage):
        job = jobs[name]
        kind, bit = job.stages[stage]
        land = job.landing[stage]
        height = job.unit
        me = b // job.fold
        k = job.sem_base + stage
        wait_bytes(land, job_recv.at[k])
        wait_bytes(land, job_sem.at[k])
        stride, start, wide = job_view(job, stage)
        last = stage == len(job.stages) - 1
        if kind in ("batch", "cut"):
            if kind == "batch":
                stride = 2 * bit
            else:
                wide //= 2
                start = start + bit_of(s, bit) * wide

            def body(t, _):
                row = lax.rem(me, stride) + t * stride
                at = pl.ds(aligned(row * height, height), height)
                cols = pl.ds(aligned(start, PAIR), wide)
                from_there = land[pl.ds(aligned(t * height, height), height), :].astype(F32)
                job.grad[at, cols] = (job.grad[at, cols].astype(F32) + from_there).astype(BF)
                return 0

            lax.fori_loop(0, job.units // stride, body, 0)
        elif kind in ("add", "fold"):
            at = pl.ds(aligned(me * height, height), height)
            cols = pl.ds(start, wide)
            total = job.grad[at, cols].astype(F32) + land[...].astype(F32)
            if last:
                mine = total[: job.row_block]
                for n in range(1, job.fold):
                    here = total[n * job.row_block : (n + 1) * job.row_block]
                    mine = jnp.where(lax.rem(b, job.fold) == n, here, mine)
                job.out[:, cols] = mine
            else:
                job.grad[at, cols] = total.astype(BF)
        else:
            start, wide = gather_view(job, stage)
            at = pl.ds(aligned(me * height, height), height)
            theirs = start + (1 - 2 * bit_of(s, bit)) * wide
            if last:
                cols = pl.ds(aligned(start, PAIR), wide)
                job.out[:, cols] = job.grad[at, cols].astype(F32)
                job.out[:, pl.ds(aligned(theirs, PAIR), wide)] = land[...].astype(F32)
            else:
                job.grad[at, pl.ds(aligned(theirs, PAIR), wide)] = land[...]
        if not last:
            job_start(name, stage + 1)

    step = width

    def feed_back(i, _):
        at = pl.ds(aligned(i * step, step), step)
        grad_hidden = dot(gbf[...], down[at, :], 1, 1)
        grad_pre = (grad_hidden * slope[:, at].astype(F32)).astype(BF)
        down[at, :] = dot(hidden[:, at], gbf[...], 0, 0).astype(BF)
        hidden[:, at] = grad_pre
        return 0

    lax.fori_loop(0, hidden_width // step, feed_back, 0)
    job_start("down_y", 0)
    job_start("down_x", 0)

    def feed_back_in(i, _):
        at = pl.ds(aligned(i * ITER, ITER), ITER)
        gx[:, at] = dot(hidden[...], up[at, :], 1, 1)
        return 0

    lax.fori_loop(0, iters, feed_back_in, 0)
    job_finish("down_y", 0)
    job_finish("down_x", 0)

    def feed_up_grad(i, _):
        at = pl.ds(aligned(i * step, step), step)
        up[:, at] = dot(b_in[...], hidden[:, at], 0, 0).astype(BF)
        return 0

    lax.fori_loop(0, hidden_width // step, feed_up_grad, 0)
    job_start("up_y", 0)
    job_start("up_x", 0)

    def middle_rows(i, sums):
        at = pl.ds(aligned(i * ROWS_LN, ROWS_LN), ROWS_LN)
        normed, inverse = normalize(x1[at, :])
        grad_in = gx[at, :]
        made = cot[at, :].astype(F32) + norm_back(
            grad_in * (1.0 + piece_of(SCALE_FEED)), normed, inverse
        )
        gx[at, :] = made
        gbf[at, :] = (piece_of(GATE_MIX) * made).astype(BF)
        return (
            sums[0] + col_sum(grad_in),
            sums[1] + col_sum(grad_in * normed),
            sums[2] + col_sum(made * branch[at, :].astype(F32)),
        )

    zero = jnp.zeros((1, width), F32)
    sums = lax.fori_loop(0, rows // ROWS_LN, middle_rows, (zero, zero, zero))
    for index, total in zip((SHIFT_FEED, SCALE_FEED, GATE_MIX), sums):
        mod[1:2, pl.ds(index * width, width)] = total

    def project_back(i, _):
        at = pl.ds(aligned(i * ITER, ITER), ITER)
        dout[:, at] = dot(gbf[...], project[at, :], 1, 1).astype(BF)
        return 0

    lax.fori_loop(0, iters, project_back, 0)
    project[...] = dot(mixed[...], gbf[...], 0, 0).astype(BF)
    job_start("project", 0)
    job_finish("up_y", 0)
    job_finish("up_x", 0)
    x1[...] = jnp.zeros_like(x1)

    def dkv_copy(i):
        at = pl.ds(aligned(i * 2 * ITER, 2 * ITER), 2 * ITER)
        there = pl.ds(aligned(2 * width + i * 2 * ITER, 2 * ITER), 2 * ITER)
        return to_core(slope.at[:, at], slope.at[:, there], dkv_sem, dkv_recv, i)

    def attend_back(i):
        for inner in range(2):
            pair = 2 * i + inner
            at = pl.ds(aligned(pair * PAIR, PAIR), PAIR)
            at_v = pl.ds(aligned(width + pair * PAIR, PAIR), PAIR)
            query, grads = q[:, at], dout[:, at]
            key = jnp.concatenate([kv[:, at], kv_other[1, :, at]], axis=0)
            value = jnp.concatenate([kv[:, at_v], kv_other[1, :, at_v]], axis=0)
            crossed = grads.astype(F32) * mixed[:, at].astype(F32)
            lane_q, lane_k = lanes(query.shape), lanes(key.shape)
            dq = dk = dv = None
            for head in range(2):
                spare = HEAD * (1 - head)
                query_h, grads_h = one_head(query, head), one_head(grads, head)
                key_h = one_head(key, head)
                level = jnp.sum(
                    jnp.where(lanes(lse.shape) == 2 * pair + head, lse[...], 0.0),
                    axis=1,
                    keepdims=True,
                )
                delta = jnp.sum(one_head(crossed, head), axis=1, keepdims=True)
                scaled = query_h.astype(F32) * EXP_SCALE
                high = scaled.astype(BF)
                low = (scaled - high.astype(F32)).astype(BF)
                level1 = (-level).astype(BF)
                left = -level - level1.astype(F32)
                level2 = left.astype(BF)
                level3 = (left - level2.astype(F32)).astype(BF)
                low = jnp.where(lane_q == spare, level1, low)
                low = jnp.where(lane_q == spare + 1, level2, low)
                low = jnp.where(lane_q == spare + 2, level3, low)
                key_low = jnp.where(
                    jnp.logical_and(lane_k >= spare, lane_k < spare + 3),
                    jnp.ones_like(key),
                    key_h,
                )
                probs = jnp.exp2(
                    dot(
                        jnp.concatenate([high, low], axis=1),
                        jnp.concatenate([key_h, key_low], axis=1),
                        1,
                        1,
                    )
                )
                delta1 = (-delta).astype(BF)
                delta2 = (-delta - delta1.astype(F32)).astype(BF)
                grads_d = jnp.where(lane_q == spare, delta1, grads_h)
                grads_d = jnp.where(lane_q == spare + 1, delta2, grads_d)
                value_d = jnp.where(
                    jnp.logical_and(lane_k >= spare, lane_k < spare + 2),
                    jnp.ones_like(value),
                    value,
                )
                grad_scores = (probs * dot(grads_d, value_d, 1, 1)).astype(BF)
                dv_h = dot(probs.astype(BF), grads_h, 0, 0)
                dk_h = dot(grad_scores, query_h, 0, 0)
                dq_h = dot(grad_scores, key_h)
                if head == 0:
                    dq, dk, dv = dq_h, dk_h, dv_h
                else:
                    dq, dk, dv = dq + dq_h, dk + dk_h, dv + dv_h
            hidden[:, pl.ds(aligned(i * block + inner * PAIR, PAIR), PAIR)] = rotate(
                dq * SCALE, -1.0
            ).astype(BF)
            for part, made in ((0, dk * SCALE), (1, dv)):
                off = part * ITER + inner * PAIR
                dkv[lax.rem(i, 2), :, pl.ds(off, PAIR)] = made[:rows]
                slope[:, pl.ds(aligned(i * 2 * ITER + off, PAIR), PAIR)] = made[rows:].astype(BF)

    def attend_finish(i):
        copy = dkv_copy(i)
        copy.wait()
        there = 2 * width + i * 2 * ITER
        dk = dkv[i % 2, :, 0:ITER] + slope[:, pl.ds(there, ITER)].astype(F32)
        dv = dkv[i % 2, :, ITER : 2 * ITER] + slope[:, pl.ds(there + ITER, ITER)].astype(F32)
        hidden[:, pl.ds(i * block + ITER, ITER)] = rotate(dk, -1.0).astype(BF)
        hidden[:, pl.ds(i * block + 2 * ITER, ITER)] = dv.astype(BF)
        here = pl.ds(i * block, block)
        x1[...] += dot(hidden[:, here], mix[:, here], 1, 1)
        mix[:, here] = dot(a_in[...], hidden[:, here], 0, 0).astype(BF)
        job_start(f"mix{i}_x", 0)
        job_start(f"mix{i}_y", 0)

    def attend_step(i, _):
        attend_back(i)
        dkv_copy(i).start()

        @pl.when(i == 0)
        def _():
            job_finish("project", 0)
            job_finish("down_x", 1)
            job_finish("down_y", 1)

        for done in range(1, iters):

            @pl.when(i == done)
            def _():
                attend_finish(done - 1)
                if done == 1:
                    job_finish("down_x", 2)
                    job_finish("down_y", 2)
                    job_finish("up_x", 1)
                if done == 2:
                    job_finish("up_y", 1)
                    job_finish("down_x", 3)
                    job_finish("down_y", 3)
                    job_finish("up_x", 2)
                    job_finish("mix0_x", 0)
                    job_finish("mix0_y", 0)
                    job_finish("project", 1)

        return 0

    lax.fori_loop(0, iters, attend_step, 0)
    attend_finish(iters - 1)
    finished = {
        "down_x": 3, "down_y": 3, "up_x": 2, "up_y": 1, "project": 1, "mix0_x": 0, "mix0_y": 0
    }

    def last_rows(i, sums):
        at = pl.ds(aligned(i * ROWS_LN, ROWS_LN), ROWS_LN)
        normed, inverse = normalize(x[at, :])
        grad_in = x1[at, :]
        made = gx[at, :] + norm_back(grad_in * (1.0 + piece_of(SCALE_MIX)), normed, inverse)
        gbf[at, :] = made.astype(BF)
        return sums[0] + col_sum(grad_in), sums[1] + col_sum(grad_in * normed)

    sums = lax.fori_loop(0, rows // ROWS_LN, last_rows, (zero, zero))
    share_start(rows_of(gbf), seq_of(igrad_hbm), 3)
    for index, total in zip((SHIFT_MIX, SCALE_MIX), sums):
        mod[1:2, pl.ds(index * width, width)] = total

    strips = width // 128
    for strip in range(6 * strips):
        gsum[strip : strip + 1, :] = mod[1:2, strip * 128 : (strip + 1) * 128]
    for strip in range(strips):
        gsum[6 * strips + strip : 6 * strips + strip + 1, :] = code[
            :, strip * 128 : (strip + 1) * 128
        ]
    gsum[7 * strips :, :] = jnp.zeros_like(gsum[7 * strips :, :])
    gcopy = to_core(gsum, gsum_other, small_sem, small_recv, 1)
    gcopy.start()
    gcopy.wait()
    line_ids = lax.broadcasted_iota(jnp.int32, gsum.shape, 0)
    chip = b // 2
    gsum_other[...] = jnp.where(line_ids < 6 * strips, gsum[...] + gsum_other[...], gsum[...])
    keep = pltpu.make_async_copy(
        gsum_other, out_all.at[chip * seq_count + s], small_recv.at[0]
    )
    keep.start()
    keep.wait()

    def gather_copies():
        k = 2
        copies = []
        for bit in bits_of(seq_count):
            start = chip * seq_count + (s // bit) * bit
            copies.append((start, bit, (flip(s, bit), b)))
        for bit in bits_of(batch_count)[1:]:
            chips = bit // 2
            start = (chip // chips) * chips * seq_count
            copies.append((start, chips * seq_count, (s, flip(b, bit))))
        made = []
        for start, count, peer in copies:
            ref = out_all.at[pl.ds(start, count)]
            made.append(
                pltpu.make_async_remote_copy(
                    src_ref=ref,
                    dst_ref=ref,
                    send_sem=small_sem.at[k],
                    recv_sem=small_recv.at[k],
                    device_id=peer,
                    device_id_type=MESH,
                )
            )
            k += 1
        return made

    gathers = gather_copies()
    gathers[0].start()

    order = []
    longest = max(len(job.stages) for job in jobs.values())
    for late in range(longest + 12):
        for n, name in enumerate(jobs):
            stage = late - n // 2
            if finished.get(name, -1) < stage < len(jobs[name].stages) and stage >= 0:
                order.append((name, stage))
    gather_done = 0
    for n, (name, stage) in enumerate(order):
        job_finish(name, stage)
        if n % 4 == 3 and gather_done < len(gathers):
            gathers[gather_done].wait()
            gather_done += 1
            if gather_done < len(gathers):
                gathers[gather_done].start()
    while gather_done < len(gathers):
        gathers[gather_done].wait()
        gather_done += 1
        if gather_done < len(gathers):
            gathers[gather_done].start()
    wait_bytes(layer_hbm, share_recv.at[2])
    share_sent(rows_of(x16), seq_of(layer_hbm), 2)
    wait_bytes(igrad_hbm, share_recv.at[3])
    share_sent(rows_of(gbf), seq_of(igrad_hbm), 3)


def per_device(sizes, inputs, cotangent, cond_mask, timestep, embed_table, mix_weight,
               project_weight, up_weight, down_weight, cond_weight, cond_bias):
    seq_count, batch_count = sizes
    seqs_here, pos_here, width = inputs.shape
    hidden_width = up_weight.shape[1]
    length = pos_here * seq_count
    rows = seqs_here * pos_here
    code_rows = -(-seqs_here // 8) * 8
    pad = code_rows - seqs_here
    code = jax.nn.silu(embed_table[timestep]).astype(BF).astype(F32)
    flags = jnp.broadcast_to(cond_mask.astype(F32)[:, None], code.shape)
    codes = jnp.concatenate(
        [jnp.pad(code, ((0, pad), (0, 0))), jnp.pad(flags, ((0, pad), (0, 0)))], axis=0
    )
    cosine, sine = rotary_constants(length)
    shares = [
        jax.ShapeDtypeStruct((weight.shape[0] // batch_count, weight.shape[1]), F32)
        for weight in (mix_weight, project_weight, up_weight, down_weight)
    ]
    total = batch_count * seqs_here
    lines = -(-7 * (width // 128) // 8) * 8
    shells = [
        jax.ShapeDtypeStruct(weight.shape, BF)
        for weight in (down_weight, up_weight, project_weight, mix_weight)
    ]
    landings, sem_count = [], 0
    for job in job_list(shells, [None] * 4, sizes).values():
        landings += [pltpu.VMEM(shape, BF) for shape in job.landing_shapes()]
        sem_count += len(job.stages)
    vmem = pl.BlockSpec(memory_space=pltpu.VMEM)
    hbm = pl.BlockSpec(memory_space=pl.ANY)
    wide = (rows, width)
    smalls = 1 + len(bits_of(seq_count)) + len(bits_of(batch_count))
    dma = pltpu.SemaphoreType.DMA
    layer, igrad, share_mix, share_project, share_up, share_down, gall = pl.pallas_call(
        functools.partial(step_kernel, sizes, seqs_here, pos_here),
        name="block_step",
        out_shape=[
            jax.ShapeDtypeStruct(inputs.shape, BF),
            jax.ShapeDtypeStruct(inputs.shape, BF),
            *shares,
            jax.ShapeDtypeStruct((total, lines, 128), F32),
        ],
        in_specs=[hbm, hbm, vmem, vmem] + [hbm] * 7,
        out_specs=[hbm, hbm] + [vmem] * 4 + [vmem if total <= 32 else hbm],
        scratch_shapes=[
            pltpu.VMEM(mix_weight.shape, BF),
            pltpu.VMEM(project_weight.shape, BF),
            pltpu.VMEM(up_weight.shape, BF),
            pltpu.VMEM(down_weight.shape, BF),
            pltpu.VMEM((rows, PAIR), F32),
            pltpu.VMEM((rows, PAIR), F32),
            pltpu.VMEM(wide, BF),
            pltpu.VMEM(wide, BF),
            pltpu.VMEM(wide, F32),
            pltpu.VMEM(wide, F32),
            pltpu.VMEM(wide, BF),
            pltpu.VMEM(wide, BF),
            pltpu.VMEM((rows, 2 * width), BF),
            pltpu.VMEM((2, rows, 2 * width), BF),
            pltpu.VMEM(wide, BF),
            pltpu.VMEM(wide, BF),
            pltpu.VMEM(wide, BF),
            pltpu.VMEM((rows, hidden_width), BF),
            pltpu.VMEM((rows, hidden_width), BF),
            pltpu.VMEM(wide, BF),
            pltpu.VMEM(wide, F32),
            pltpu.VMEM(wide, BF),
            pltpu.VMEM((2, rows, 2 * ITER), F32),
            pltpu.VMEM((rows, 128), F32),
            pltpu.VMEM((8, 6 * width), F32),
            pltpu.VMEM(codes.shape, F32),
            pltpu.VMEM((lines, 128), F32),
            pltpu.VMEM((lines, 128), F32),
            landings,
            dma((9,)),
            dma((4,)),
            dma((4,)),
            dma((4,)),
            dma((4,)),
            dma((width // ITER,)),
            dma((width // ITER,)),
            dma((smalls,)),
            dma((smalls,)),
            dma((sem_count,)),
            dma((sem_count,)),
        ],
        compiler_params=pltpu.CompilerParams(
            collective_id=0, has_side_effects=True, vmem_limit_bytes=VMEM_BYTES
        ),
    )(
        inputs,
        cotangent,
        codes,
        cond_bias[None, :],
        jnp.asarray(cosine),
        jnp.asarray(sine),
        mix_weight,
        project_weight,
        up_weight,
        down_weight,
        cond_weight,
    )
    share_mix = (
        share_mix.reshape(share_mix.shape[0], width // ITER, 3, ITER)
        .transpose(0, 2, 1, 3)
        .reshape(share_mix.shape)
    )
    strips = width // 128
    grad_mod = gall[:, : 6 * strips].reshape(total, 6 * width)
    codes_all = gall[:, 6 * strips : 7 * strips].reshape(total, width)
    me = lax.axis_index("batch")
    code_rows_here = lax.dynamic_slice_in_dim(
        codes_all, me * (width // batch_count), width // batch_count, 1
    )
    share_cond = jnp.dot(code_rows_here.T, grad_mod, precision=lax.Precision.HIGHEST)
    share_bias = jnp.sum(
        lax.dynamic_slice_in_dim(
            grad_mod, me * (6 * width // batch_count), 6 * width // batch_count, 1
        ),
        axis=0,
    )
    return (
        layer,
        igrad.astype(F32),
        share_mix,
        share_project,
        share_up,
        share_down,
        share_cond,
        share_bias,
    )


VMEM_BYTES = 64 * 1024 * 1024 - 512 * 1024


def solution(mesh):
    sizes = (mesh.shape["seq"], mesh.shape["batch"])
    split = P("batch", "seq", None)
    placed = (split, split, P("batch"), P("batch")) + (P(),) * 7
    return jax.shard_map(
        functools.partial(per_device, sizes),
        mesh=mesh,
        in_specs=placed,
        out_specs=(split, split) + (P("batch", None),) * 5 + (P("batch"),),
        check_vma=False,
    )
```

```python
import functools
import math

import jax
import jax.numpy as jnp
import numpy as np
from jax import lax
from jax.experimental import pallas as pl
from jax.experimental.pallas import tpu as pltpu
from jax.sharding import PartitionSpec as P

HEAD = 64
PAIR = 2 * HEAD
ITER = 2 * PAIR
EPS = 1e-06
THETA = 10000.0
LOG2E = 1.4426950408889634
SCALE = HEAD ** (-0.5)
EXP_SCALE = SCALE * LOG2E
GELU_A = math.sqrt(2.0 / math.pi)
GELU_B = 0.044715
BF = jnp.bfloat16
F32 = jnp.float32
MESH = pl.DeviceIdType.MESH
ROWS_LN = 256


def dot(left, right, left_dim=1, right_dim=0):
    return lax.dot_general(
        left, right, (((left_dim,), (right_dim,)), ((), ())), preferred_element_type=F32
    )


def lanes(shape):
    return lax.broadcasted_iota(jnp.int32, shape, len(shape) - 1)


def in_head(shape, head):
    return lanes(shape) >= HEAD if head else lanes(shape) < HEAD


def one_head(values, head):
    return jnp.where(in_head(values.shape, head), values, jnp.zeros_like(values))


def bit_of(value, bit):
    return lax.rem(value // bit, 2)


def flip(value, bit):
    return value + bit - 2 * bit * bit_of(value, bit)


def aligned(value, unit):
    return pl.multiple_of(value, unit)


def rotary_constants(length):
    half_size = HEAD // 2
    freqs = THETA ** (-np.arange(half_size, dtype=np.float64) * 2.0 / HEAD)
    angles = np.arange(length, dtype=np.float64)[:, None] * freqs[None, :]
    cosine, sine = np.cos(angles), np.sin(angles)
    cosine = np.concatenate([cosine] * 4, axis=1).astype(np.float32)
    sine = np.concatenate([-sine, sine] * 2, axis=1).astype(np.float32)
    return cosine, sine


def swap_halves(values):
    first = lax.rem(lanes(values.shape), HEAD) < HEAD // 2
    return jnp.where(
        first, pltpu.roll(values, PAIR - HEAD // 2, 1), pltpu.roll(values, HEAD // 2, 1)
    )


def normalize(values):
    row_mean = jnp.mean(values, axis=-1, keepdims=True)
    centered = values - row_mean
    row_var = jnp.mean(centered * centered, axis=-1, keepdims=True)
    inverse = lax.rsqrt(row_var + EPS)
    return centered * inverse, inverse


def norm_back(grad_normed, normed, inverse):
    grad_mean = jnp.mean(grad_normed, axis=-1, keepdims=True)
    cross_mean = jnp.mean(grad_normed * normed, axis=-1, keepdims=True)
    return inverse * (grad_normed - grad_mean - normed * cross_mean)


def col_sum(values):
    return jnp.sum(values, axis=0, keepdims=True)


def bits_of(count):
    return [1 << k for k in range(count.bit_length() - 1)]


def wait_bytes(ref, sem):
    pltpu.make_async_copy(ref, ref, sem).wait()


class Job:
    def __init__(self, grad, out, first, width, kind, sizes):
        self.grad, self.out, self.first, self.width = grad, out, first, width
        self.seq_count, self.batch_count = sizes
        self.row_block = grad.shape[0] // self.batch_count
        self.fold = 1
        while self.row_block * self.fold % 16:
            self.fold *= 2
        self.unit = self.row_block * self.fold
        self.units = self.batch_count // self.fold
        self.order = bits_of(self.units)
        if kind == "Z":
            self.order = self.order[:1] + self.order[2:] + self.order[1:2]
        halvings = [("batch", bit) for bit in self.order]
        if kind == "X" and self.fold == 1 and (width // self.seq_count) % PAIR == 0:
            self.stages = (
                halvings[:1]
                + [("cut", bit) for bit in bits_of(self.seq_count)]
                + halvings[1:]
                + [("gather", bit) for bit in bits_of(self.seq_count)[::-1]]
            )
        else:
            self.stages = (
                halvings
                + [("add", bit) for bit in bits_of(self.seq_count)]
                + [("fold", bit) for bit in bits_of(self.fold)]
            )

    def landing_shapes(self):
        count, width, shapes = self.units, self.width, []
        for kind, _ in self.stages:
            if kind == "batch":
                count //= 2
            elif kind == "cut":
                width //= 2
            shapes.append((count * self.unit, width))
            if kind == "gather":
                width *= 2
        return shapes


KINDS = {
    "up0": "Y",
    "up1": "Z",
    "up2": "Z",
    "up3": "Y",
    "down0": "Y",
    "down1": "X",
    "down2": "Y",
    "project": "X",
    "mix0a": "X",
    "mix0b": "Y",
    "mix1a": "X",
    "mix1b": "Y",
    "mix2a": "Y",
    "mix2b": "Y",
}


def job_list(grads, outs, sizes):
    grad_down, grad_up, grad_project, grad_mix = grads
    out_down, out_up, out_project, out_mix = outs
    model_width, hidden_width = grad_up.shape
    jobs = {}

    def add(name, grad, out, first, width):
        jobs[name] = Job(grad, out, first, width, KINDS[name], sizes)

    for i in range(hidden_width // model_width):
        add(f"up{i}", grad_up, out_up, i * model_width, model_width)
    for i in range(model_width // ITER):
        add(f"down{i}", grad_down, out_down, i * ITER, ITER)
    add("project", grad_project, out_project, 0, model_width)
    for i in range(model_width // ITER):
        add(f"mix{i}a", grad_mix, out_mix, i * 3 * ITER, 2 * ITER)
        add(f"mix{i}b", grad_mix, out_mix, i * 3 * ITER + 2 * ITER, ITER)
    return jobs


def borrows(name, stage):
    return name.startswith("mix") and stage == 0


PLAN = {
    "up0": (),
    "up1": (
        ("up0", 0),
    ),
    "up2": (
        ("up1", 0),
    ),
    "up3": (
        ("up2", 0),
    ),
    "feed": (
        ("up0", 1), ("up3", 0),
    ),
    "down": (
        ("up1", 1),
    ),
    "middle": (),
    "project": (
        ("down0", 0),
    ),
    "attend0": (
        ("up2", 1), ("down1", 0), ("up3", 1), ("down2", 0), ("up0", 2),
        ("project", 0),
    ),
    "attend1": (
        ("up1", 2), ("down0", 1),
    ),
    "mix0": (
        ("up3", 2), ("up2", 2),
    ),
    "attend2": (
        ("down1", 1), ("mix0a", 0), ("up0", 3), ("mix0b", 0), ("down2", 1),
        ("down0", 2), ("up1", 3), ("up3", 3), ("up2", 3), ("project", 1),
    ),
    "mix1": (),
    "mix2": (
        ("down1", 2), ("mix0a", 1), ("mix1a", 0), ("down2", 2), ("mix1b", 0),
        ("up0", 4), ("mix0b", 1), ("up1", 4), ("down0", 3), ("up3", 4),
        ("mix2a", 0), ("project", 2), ("mix2b", 0),
    ),
    "last": (
        ("up2", 4),
    ),
    "tail": (
        ("down1", 3), ("mix0a", 2), ("mix1b", 1), ("mix1a", 1), ("mix0b", 2),
        ("down2", 3), ("project", 3), ("down0", 4), ("down1", 4), ("mix2a", 1),
        ("mix0a", 3), ("mix1b", 2), ("mix2b", 1), ("mix0b", 3), ("project", 4),
        ("mix1a", 2), ("mix2a", 2), ("mix0a", 4), ("mix1b", 3), ("mix2b", 2),
        ("mix1a", 3), ("down2", 4), ("mix2a", 3), ("down1", 5), ("mix0b", 4),
        ("mix2b", 3), ("project", 5), ("mix1a", 4), ("mix0a", 5), ("mix1b", 4),
        ("mix2a", 4), ("mix2b", 4), ("mix1a", 5),
    ),
}


def step_kernel(
    sizes,
    seqs_here,
    pos_here,
    inputs_hbm,
    cot_hbm,
    flags_ref,
    steps_ref,
    table_hbm,
    bias_ref,
    cos_hbm,
    sin_hbm,
    mix_hbm,
    project_hbm,
    up_hbm,
    down_hbm,
    cond_hbm,
    layer_hbm,
    igrad_hbm,
    out_mix,
    out_project,
    out_up,
    out_down,
    out_early,
    out_late,
    mix,
    project,
    up,
    down,
    cos,
    sin,
    x16,
    cot,
    x,
    x1,
    a_in,
    q,
    kv,
    kv_other,
    mixed,
    branch,
    b_in,
    dkv_out,
    hidden,
    gbf,
    gx,
    dout,
    dkv,
    lse,
    mod,
    codes,
    codes_other,
    sums_early,
    sums_late,
    landings,
    load_sem,
    share_sem,
    share_recv,
    kv_sem,
    kv_recv,
    dkv_sem,
    dkv_recv,
    small_sem,
    small_recv,
    job_sem,
    job_recv,
):
    seq_count, batch_count = sizes
    out_all, sums_here = (out_early, out_late), (sums_early, sums_late)
    rows, width = x.shape
    hidden_width = up.shape[1]
    pairs = width // PAIR
    iters = width // ITER
    block = 3 * ITER
    s = lax.axis_index("seq")
    b = lax.axis_index("batch")
    core = lax.rem(b, 2)
    core_peer = (s, flip(b, 1))

    barrier = pltpu.get_barrier_semaphore()
    chip_count = batch_count // 2
    chip = b // 2
    near = [
        (lax.rem(s + n // 2, seq_count), flip(b, 1) if n % 2 else b)
        for n in range(1, 2 * seq_count)
    ]
    far = [(s, 2 * lax.rem(chip + n, chip_count) + core) for n in range(1, chip_count)]
    peers = near + far
    for peer in peers:
        pl.semaphore_signal(barrier, inc=1, device_id=peer, device_id_type=MESH)

    def share_peer(j):
        return core * seqs_here + j, b - core + s // seqs_here

    def is_self(j):
        ps, pb = share_peer(j)
        return jnp.logical_and(ps == s, pb == b)

    for j in range(seqs_here):

        @pl.when(jnp.logical_not(is_self(j)))
        def _():
            pl.semaphore_signal(barrier, inc=1, device_id=share_peer(j), device_id_type=MESH)

    own = jnp.where(s // seqs_here == core, 1, 0)

    table_size = table_hbm.shape[0]
    table_loads = []
    for n, target in enumerate((x, x1)):
        count = min(rows, table_size - n * rows)
        table_loads.append(
            pltpu.make_async_copy(
                table_hbm.at[pl.ds(n * rows, count), :],
                target.at[pl.ds(0, count), :],
                load_sem.at[9 + n],
            )
        )
        table_loads[-1].start()
    cond_up = pltpu.make_async_copy(cond_hbm.at[:, pl.ds(0, hidden_width)], up, load_sem.at[0])
    cond_up.start()
    rest = cond_hbm.shape[1] - hidden_width
    cond_down = []
    for i in range(rest // width):
        cond_down.append(
            pltpu.make_async_copy(
                cond_hbm.at[:, pl.ds(hidden_width + i * width, width)],
                down.at[pl.ds(i * width, width), :],
                load_sem.at[1 + i],
            )
        )
        cond_down[-1].start()
    mix_loads = []
    for i in range(iters):
        for part in range(3):
            mix_loads.append(
                pltpu.make_async_copy(
                    mix_hbm.at[:, pl.ds(part * width + i * ITER, ITER)],
                    mix.at[:, pl.ds(i * block + part * ITER, ITER)],
                    load_sem.at[8],
                )
            )
            mix_loads[-1].start()
    row0 = core * rows
    load_cos = pltpu.make_async_copy(
        cos_hbm.at[pl.ds(aligned(row0, 128), rows), :], cos, load_sem.at[5]
    )
    load_sin = pltpu.make_async_copy(
        sin_hbm.at[pl.ds(aligned(row0, 128), rows), :], sin, load_sem.at[6]
    )
    load_project = pltpu.make_async_copy(project_hbm, project, load_sem.at[7])
    load_cos.start()
    load_sin.start()
    load_project.start()

    pl.semaphore_wait(barrier, len(peers) + seqs_here - own)

    def share_copy(source, target, j, k):
        return pltpu.make_async_remote_copy(
            src_ref=source,
            dst_ref=target,
            send_sem=share_sem.at[k],
            recv_sem=share_recv.at[k],
            device_id=share_peer(j),
            device_id_type=MESH,
        )

    slot = lax.rem(s, seqs_here)

    def share_start(source, target, k):
        for j in range(seqs_here):

            @pl.when(is_self(j))
            def _():
                pltpu.make_async_copy(source(j), target(slot), share_recv.at[k]).start()

            @pl.when(jnp.logical_not(is_self(j)))
            def _():
                share_copy(source(j), target(slot), j, k).start()

    def share_sent(source, target, k):
        for j in range(seqs_here):

            @pl.when(jnp.logical_not(is_self(j)))
            def _():
                share_copy(source(j), target(slot), j, k).wait_send()

    def rows_of(ref):
        return lambda j: ref.at[pl.ds(aligned(j * pos_here, 16), pos_here), :]

    def seq_of(ref):
        return lambda j: ref.at[j]

    def to_core(source, target, sems, recvs, k):
        return pltpu.make_async_remote_copy(
            src_ref=source,
            dst_ref=target,
            send_sem=sems.at[k],
            recv_sem=recvs.at[k],
            device_id=core_peer,
            device_id_type=MESH,
        )

    share_start(seq_of(inputs_hbm), rows_of(x16), 0)
    for load in table_loads:
        load.wait()
    half_rows = codes.shape[0] // 2
    codes[...] = jnp.zeros_like(codes)
    for j in range(seqs_here):
        time = steps_ref[j]
        low = x[pl.ds(jnp.minimum(time, rows - 1), 1), :]
        high = x1[pl.ds(jnp.maximum(time - rows, 0), 1), :]
        embedding = jnp.where(time < rows, low, high)
        codes[j : j + 1, :] = jax.nn.silu(embedding).astype(BF).astype(F32)
        codes[half_rows + j : half_rows + j + 1, :] = jnp.full(
            (1, width), flags_ref[j].astype(F32)
        )
    code_copy = to_core(codes, codes_other, small_sem, small_recv, 0)
    code_copy.start()

    code_copy.wait()
    own_f = own.astype(F32)
    code_rows = codes[...] * own_f + codes_other[...] * (1.0 - own_f)
    row_ids = lax.broadcasted_iota(jnp.int32, code_rows.shape, 0)
    code = col_sum(jnp.where(row_ids == slot, code_rows, 0.0))
    flag = col_sum(jnp.where(row_ids == slot + half_rows, code_rows, 0.0))
    code_lhs = jnp.broadcast_to(code, (8, width)).astype(BF)
    strips = width // 128

    def bias_of(piece):
        return jnp.concatenate(
            [bias_ref[piece * strips + n : piece * strips + n + 1, :] for n in range(strips)], axis=1
        )

    cond_up.wait()
    for piece in range(hidden_width // width):
        at = slice(piece * width, (piece + 1) * width)
        mod[:, at] = dot(code_lhs, up[:, at]) + bias_of(piece)
    load_up = pltpu.make_async_copy(up_hbm, up, load_sem.at[0])
    load_up.start()
    for i in range(rest // width):
        cond_down[i].wait()
        at = slice(hidden_width + i * width, hidden_width + (i + 1) * width)
        mod[:, at] = dot(code_lhs, down[i * width : (i + 1) * width, :]) + bias_of(
            hidden_width // width + i
        )
    load_down = pltpu.make_async_copy(down_hbm, down, load_sem.at[1])
    load_down.start()

    def piece_of(index, start=0, size=None):
        size = width if size is None else size
        return mod[0:1, pl.ds(index * width + start, size)]

    SHIFT_MIX, SCALE_MIX, GATE_MIX, SHIFT_FEED, SCALE_FEED, GATE_FEED = range(6)

    def norm_rows(source, target, shift_index, scale_index):
        def body(i, _):
            at = pl.ds(aligned(i * ROWS_LN, ROWS_LN), ROWS_LN)
            normed, _ = normalize(source[at, :].astype(F32))
            target[at, :] = (
                normed * (1.0 + piece_of(scale_index)) + piece_of(shift_index)
            ).astype(BF)
            return 0

        lax.fori_loop(0, rows // ROWS_LN, body, 0)

    def rotate(values, sign):
        parts = []
        for p in range(values.shape[1] // PAIR):
            part = values[:, p * PAIR : (p + 1) * PAIR]
            parts.append(part * cos[...] + sign * (swap_halves(part) * sin[...]))
        return jnp.concatenate(parts, axis=1)

    def project_part(part, target, base):
        def body(i, _):
            made = dot(a_in[...], mix[:, pl.ds(aligned(i * block + part * ITER, ITER), ITER)])
            if part < 2:
                made = rotate(made, 1.0)
            target[:, pl.ds(aligned(base + i * ITER, ITER), ITER)] = made.astype(BF)
            return 0

        lax.fori_loop(0, iters, body, 0, unroll=True)

    def kv_copy(which, part):
        at = pl.ds(part * width, width)
        return to_core(kv.at[:, at], kv_other.at[which, :, at], kv_sem, kv_recv, 2 * which + part)

    def attend(which):
        group = pairs // 2

        def body(i, _):
            for inner in range(group):
                pair = i * group + inner
                at = pl.ds(aligned(pair * PAIR, PAIR), PAIR)
                at_v = pl.ds(aligned(width + pair * PAIR, PAIR), PAIR)
                query = q[:, at]
                key = jnp.concatenate([kv[:, at], kv_other[which, :, at]], axis=0)
                value = jnp.concatenate([kv[:, at_v], kv_other[which, :, at_v]], axis=0)
                outs = []
                for head in range(2):
                    scores = dot(one_head(query, head), key, 1, 1)
                    top = jnp.max(scores, axis=1, keepdims=True)
                    weights = jnp.exp2((scores - top) * EXP_SCALE)
                    ones = jnp.where(in_head(value.shape, head), value, jnp.ones_like(value))
                    made = dot(weights.astype(BF), ones)
                    total = made[:, HEAD * (1 - head) : HEAD * (1 - head) + 1]
                    outs.append(made * (1.0 / total))
                    if which == 1:
                        level = top * EXP_SCALE + jnp.log2(total)
                        lse[...] = jnp.where(
                            lanes(lse.shape) == 2 * pair + head, level, lse[...]
                        )
                mixed[:, at] = jnp.where(
                    lanes(outs[0].shape) < HEAD, outs[0], outs[1]
                ).astype(BF)
            return 0

        lax.fori_loop(0, 2, body, 0)

    def forward(which):
        if which == 0:
            wait_bytes(x16, share_recv.at[0])
            share_start(seq_of(cot_hbm), rows_of(cot), 1)
        norm_rows(x16 if which == 0 else x, a_in, SHIFT_MIX, SCALE_MIX)
        if which == 0:
            for load in mix_loads:
                load.wait()
            load_cos.wait()
            load_sin.wait()
        project_part(1, kv, 0)
        key_copy = kv_copy(which, 0)
        key_copy.start()
        project_part(2, kv, width)
        value_copy = kv_copy(which, 1)
        value_copy.start()
        project_part(0, q, 0)
        key_copy.wait()
        value_copy.wait()
        attend(which)
        if which == 0:
            load_project.wait()

        def mix_out(i, _):
            at = pl.ds(aligned(i * ITER, ITER), ITER)
            made = dot(mixed[...], project[:, at])
            if which == 1:
                branch[:, at] = made.astype(BF)
            base = x16[:, at].astype(F32) if which == 0 else x[:, at]
            gate = mod[0:1, pl.ds(aligned(GATE_MIX * width + i * ITER, ITER), ITER)]
            x1[:, at] = base + gate * made
            return 0

        lax.fori_loop(0, iters, mix_out, 0, unroll=True)
        norm_rows(x1, b_in, SHIFT_FEED, SCALE_FEED)
        if which == 0:
            load_up.wait()
        if which == 1:
            return
        step = 2 * ITER

        def feed_up(i, _):
            at = pl.ds(aligned(i * step, step), step)
            pre = dot(b_in[...], up[:, at])
            inner = jnp.tanh(pre * (GELU_A + (GELU_A * GELU_B) * (pre * pre)))
            hidden[:, at] = (pre * (0.5 * (1.0 + inner))).astype(BF)
            return 0

        lax.fori_loop(0, hidden_width // step, feed_up, 0, unroll=3)
        load_down.wait()

        def feed_down(i, _):
            at = pl.ds(aligned(i * ITER, ITER), ITER)
            gate = mod[0:1, pl.ds(aligned(GATE_FEED * width + i * ITER, ITER), ITER)]
            result = x1[:, at] + gate * dot(hidden[...], down[:, at])
            x[:, at] = x16[:, at].astype(F32) + flag[:, 0:1] * result
            return 0

        lax.fori_loop(0, iters, feed_down, 0, unroll=True)

    forward(0)
    share_sent(seq_of(inputs_hbm), rows_of(x16), 0)
    wait_bytes(cot, share_recv.at[1])
    share_sent(seq_of(cot_hbm), rows_of(cot), 1)
    forward(1)

    jobs = job_list((down, up, project, mix), (out_down, out_up, out_project, out_mix), sizes)
    spare, sem_at = list(landings), 0
    for name, job in jobs.items():
        job.landing = []
        for stage in range(len(job.stages)):
            if borrows(name, stage):
                lender = jobs["up" + name[3]].landing[0]
                job.landing.append(lender.at[:, pl.ds(job.first % block, job.width)])
            else:
                job.landing.append(spare.pop(0))
        job.sem_base = sem_at
        sem_at += len(job.stages)

    def job_view(job, stage):
        me = b // job.fold
        row, height, start, wide = 0, job.units * job.unit, job.first, job.width
        for kind, bit in job.stages[:stage]:
            if kind == "batch":
                height //= 2
                row = row + bit_of(me, bit) * height
            elif kind == "cut":
                wide //= 2
                start = start + bit_of(s, bit) * wide
        return row, height, start, wide

    def gather_view(job, stage):
        start, wide = job.first, job.width
        done = [bit for kind, bit in job.stages[:stage] if kind == "gather"]
        for kind, bit in job.stages:
            if kind == "cut" and bit not in done:
                wide //= 2
                start = start + bit_of(s, bit) * wide
        return start, wide

    def job_copy(job, stage):
        kind, bit = job.stages[stage]
        row, height, start, wide = job_view(job, stage)
        peer = (flip(s, bit), b)
        if kind == "batch":
            height //= 2
            row = row + (1 - bit_of(b // job.fold, bit)) * height
            peer = (s, flip(b, bit * job.fold))
        elif kind == "cut":
            wide //= 2
            start = start + (1 - bit_of(s, bit)) * wide
        elif kind == "gather":
            start, wide = gather_view(job, stage)
        elif kind == "fold":
            peer = (s, flip(b, bit))
        return pltpu.make_async_remote_copy(
            src_ref=job.grad.at[
                pl.ds(aligned(row, job.unit), height), pl.ds(aligned(start, PAIR), wide)
            ],
            dst_ref=job.landing[stage],
            send_sem=job_sem.at[job.sem_base + stage],
            recv_sem=job_recv.at[job.sem_base + stage],
            device_id=peer,
            device_id_type=MESH,
        )

    def job_start(name, stage):
        job_copy(jobs[name], stage).start()

    def job_finish(name, stage):
        job = jobs[name]
        kind, bit = job.stages[stage]
        land = job.landing[stage]
        job_copy(job, stage).wait()
        last = stage == len(job.stages) - 1
        row, height, start, wide = job_view(job, stage + 1)
        at = pl.ds(aligned(row, job.unit), height)
        cols = pl.ds(aligned(start, PAIR), wide)
        if kind in ("batch", "cut"):

            def body(t, _):
                here = pl.ds(aligned(row + t * job.unit, job.unit), job.unit)
                there = pl.ds(aligned(t * job.unit, job.unit), job.unit)
                job.grad[here, cols] = job.grad[here, cols] + land[there, :]
                return 0

            lax.fori_loop(0, height // job.unit, body, 0)
        elif kind in ("add", "fold"):
            total = job.grad[at, cols].astype(F32) + land[...].astype(F32)
            if last:
                mine = total[: job.row_block]
                for n in range(1, job.fold):
                    here = total[n * job.row_block : (n + 1) * job.row_block]
                    mine = jnp.where(lax.rem(b, job.fold) == n, here, mine)
                job.out[:, cols] = mine.astype(BF)
            else:
                job.grad[at, cols] = total.astype(BF)
        else:
            start, wide = gather_view(job, stage)
            cols = pl.ds(aligned(start, PAIR), wide)
            theirs = pl.ds(aligned(start + (1 - 2 * bit_of(s, bit)) * wide, PAIR), wide)
            if last:
                job.out[:, cols] = job.grad[at, cols]
                job.out[:, theirs] = land[...]
            else:
                job.grad[at, theirs] = land[...]
        if not last:
            job_start(name, stage + 1)

    def spread_near(k):
        place = 2 * s + core
        return [
            pltpu.make_async_remote_copy(
                src_ref=sums_here[k].at[place],
                dst_ref=sums_here[k].at[place],
                send_sem=small_sem.at[2 * k + 1],
                recv_sem=small_recv.at[2 * k + 1],
                device_id=peer,
                device_id_type=MESH,
            )
            for peer in near
        ]

    def spread_far(k):
        here = out_all[k].at[pl.ds(chip * seq_count, seq_count)]
        return [
            pltpu.make_async_remote_copy(
                src_ref=here,
                dst_ref=here,
                send_sem=small_sem.at[2 * k + 2],
                recv_sem=small_recv.at[2 * k + 2],
                device_id=peer,
                device_id_type=MESH,
            )
            for peer in far
        ]

    def spread_start(k, pieces, tail):
        place = 2 * s + core
        line = 0
        for index in pieces:
            for strip in range(strips):
                at = slice(index * width + strip * 128, index * width + (strip + 1) * 128)
                sums_here[k][place, line : line + 1, :] = mod[1:2, at]
                line += 1
        if tail is not None:
            for strip in range(strips):
                sums_here[k][place, line : line + 1, :] = 0.5 * tail[
                    :, strip * 128 : (strip + 1) * 128
                ]
                line += 1
        left = sums_here[k].shape[1] - line
        if left:
            sums_here[k][place, line:, :] = jnp.zeros((left, 128), F32)
        for copy in spread_near(k):
            copy.start()

    def spread_pass(k):
        count = 2 * seq_count - 1
        wait_bytes(sums_here[k].at[pl.ds(0, count)], small_recv.at[2 * k + 1])
        wait_bytes(sums_here[k].at[pl.ds(0, count)], small_sem.at[2 * k + 1])
        for n in range(seq_count):
            sums_here[k][2 * n] = sums_here[k][2 * n] + sums_here[k][2 * n + 1]
            keep = pltpu.make_async_copy(
                sums_here[k].at[2 * n], out_all[k].at[chip * seq_count + n], load_sem.at[9 + n % 2]
            )
            keep.start()
            keep.wait()
        for copy in spread_far(k):
            copy.start()

    def spread_end(k):
        count = (chip_count - 1) * seq_count
        wait_bytes(out_all[k].at[pl.ds(0, count)], small_recv.at[2 * k + 2])
        wait_bytes(out_all[k].at[pl.ds(0, count)], small_sem.at[2 * k + 2])

    finished = set()

    def point(name):
        for entry in PLAN[name]:
            job_finish(*entry)
            finished.add(entry)

    def store_units(job, first, made):
        cols = slice(job.first, job.first + job.width)
        for n in range(made.shape[0] // job.unit):
            place = 0
            for bit in job.order:
                place = 2 * place + (first // job.unit + n) // bit % 2
            place *= job.unit
            job.grad[place : place + job.unit, cols] = made[
                n * job.unit : (n + 1) * job.unit
            ].astype(BF)

    for i in range(iters):
        at = slice(i * ITER, (i + 1) * ITER)
        gate = piece_of(GATE_FEED, i * ITER, ITER)
        gbf[:, at] = (gate * cot[:, at].astype(F32)).astype(BF)
    for i in range(hidden_width // width):
        at = slice(i * width, (i + 1) * width)
        pre = dot(b_in[...], up[:, at])
        square = pre * pre
        inner = jnp.tanh(pre * (GELU_A + (GELU_A * GELU_B) * square))
        left = 0.5 * (1.0 + inner)
        hidden[:, at] = (pre * left).astype(BF)
        bend = GELU_A + (3.0 * GELU_A * GELU_B) * square
        slope = left + (0.5 * pre) * (1.0 - inner * inner) * bend
        grad_pre = (dot(gbf[...], down[at, :], 1, 1) * slope).astype(BF)
        grad_in = dot(grad_pre, up[:, at], 1, 1)
        gx[...] = grad_in if i == 0 else gx[...] + grad_in
        store_units(jobs[f"up{i}"], 0, dot(b_in[...], grad_pre, 0, 0))
        job_start(f"up{i}", 0)
        if i > 0:
            point(f"up{i}")
    for i in range(iters):
        at = slice(i * ITER, (i + 1) * ITER)
        made = dot(hidden[...], down[:, at])
        x16[:, at] = (x1[:, at] + piece_of(GATE_FEED, i * ITER, ITER) * made).astype(BF)
        mod[1:2, pl.ds(GATE_FEED * width + i * ITER, ITER)] = col_sum(
            cot[:, at].astype(F32) * made
        )
    point("feed")
    for i in range(hidden_width // width):
        at = slice(i * width, (i + 1) * width)
        made = dot(hidden[:, at], gbf[...], 0, 0)
        for j in range(iters):
            store_units(jobs[f"down{j}"], i * width, made[:, j * ITER : (j + 1) * ITER])
    for i in range(iters):
        job_start(f"down{i}", 0)
    point("down")

    def middle_rows(i, sums):
        at = pl.ds(aligned(i * ROWS_LN, ROWS_LN), ROWS_LN)
        normed, inverse = normalize(x1[at, :])
        grad_in = gx[at, :]
        made = cot[at, :].astype(F32) + norm_back(
            grad_in * (1.0 + piece_of(SCALE_FEED)), normed, inverse
        )
        gx[at, :] = made
        gbf[at, :] = (piece_of(GATE_MIX) * made).astype(BF)
        return (
            sums[0] + col_sum(grad_in),
            sums[1] + col_sum(grad_in * normed),
            sums[2] + col_sum(made * branch[at, :].astype(F32)),
        )

    zero = jnp.zeros((1, width), F32)
    sums = lax.fori_loop(0, rows // ROWS_LN, middle_rows, (zero, zero, zero))
    for index, total in zip((SHIFT_FEED, SCALE_FEED, GATE_MIX), sums):
        mod[1:2, pl.ds(index * width, width)] = total
    share_start(rows_of(x16), seq_of(layer_hbm), 2)
    point("middle")

    def project_back(i, _):
        at = pl.ds(aligned(i * ITER, ITER), ITER)
        dout[:, at] = dot(gbf[...], project[at, :], 1, 1).astype(BF)
        return 0

    lax.fori_loop(0, iters, project_back, 0, unroll=True)
    store_units(jobs["project"], 0, dot(mixed[...], gbf[...], 0, 0))
    job_start("project", 0)
    spread_start(0, (GATE_MIX, SHIFT_FEED, SCALE_FEED, GATE_FEED), code)
    point("project")
    x1[...] = jnp.zeros_like(x1)

    def dkv_copy(i):
        at = pl.ds(aligned(i * 2 * ITER, 2 * ITER), 2 * ITER)
        return to_core(dkv_out.at[:, at], kv_other.at[0, :, at], dkv_sem, dkv_recv, i)

    def attend_back(i):
        for inner in range(2):
            pair = 2 * i + inner
            at = pl.ds(aligned(pair * PAIR, PAIR), PAIR)
            at_v = pl.ds(aligned(width + pair * PAIR, PAIR), PAIR)
            query, grads = q[:, at], dout[:, at]
            key = jnp.concatenate([kv[:, at], kv_other[1, :, at]], axis=0)
            value = jnp.concatenate([kv[:, at_v], kv_other[1, :, at_v]], axis=0)
            crossed = grads.astype(F32) * mixed[:, at].astype(F32)
            lane_q, lane_k = lanes(query.shape), lanes(key.shape)
            dq = dk = dv = None
            for head in range(2):
                spare = HEAD * (1 - head)
                query_h, grads_h = one_head(query, head), one_head(grads, head)
                key_h = one_head(key, head)
                level = jnp.sum(
                    jnp.where(lanes(lse.shape) == 2 * pair + head, lse[...], 0.0),
                    axis=1,
                    keepdims=True,
                )
                delta = jnp.sum(one_head(crossed, head), axis=1, keepdims=True)
                scaled = query_h.astype(F32) * EXP_SCALE
                high = scaled.astype(BF)
                low = (scaled - high.astype(F32)).astype(BF)
                level1 = (-level).astype(BF)
                left = -level - level1.astype(F32)
                level2 = left.astype(BF)
                level3 = (left - level2.astype(F32)).astype(BF)
                low = jnp.where(lane_q == spare, level1, low)
                low = jnp.where(lane_q == spare + 1, level2, low)
                low = jnp.where(lane_q == spare + 2, level3, low)
                key_low = jnp.where(
                    jnp.logical_and(lane_k >= spare, lane_k < spare + 3),
                    jnp.ones_like(key),
                    key_h,
                )
                probs = jnp.exp2(
                    dot(
                        jnp.concatenate([high, low], axis=1),
                        jnp.concatenate([key_h, key_low], axis=1),
                        1,
                        1,
                    )
                )
                delta1 = (-delta).astype(BF)
                delta2 = (-delta - delta1.astype(F32)).astype(BF)
                grads_d = jnp.where(lane_q == spare, delta1, grads_h)
                grads_d = jnp.where(lane_q == spare + 1, delta2, grads_d)
                value_d = jnp.where(
                    jnp.logical_and(lane_k >= spare, lane_k < spare + 2),
                    jnp.ones_like(value),
                    value,
                )
                grad_scores = (probs * dot(grads_d, value_d, 1, 1)).astype(BF)
                dv_h = dot(grads_h, probs.astype(BF), 0, 0)
                dk_h = dot(query_h, grad_scores, 0, 0)
                dq_h = dot(grad_scores, key_h)
                if head == 0:
                    dq, dk, dv = dq_h, dk_h, dv_h
                else:
                    dq, dk, dv = dq + dq_h, dk + dk_h, dv + dv_h
            hidden[:, pl.ds(aligned(i * block + inner * PAIR, PAIR), PAIR)] = rotate(
                dq * SCALE, -1.0
            ).astype(BF)
            for part, made in ((0, dk.T * SCALE), (1, dv.T)):
                off = part * ITER + inner * PAIR
                dkv[lax.rem(i, 2), :, pl.ds(off, PAIR)] = made[:rows]
                dkv_out[:, pl.ds(aligned(i * 2 * ITER + off, PAIR), PAIR)] = made[rows:].astype(BF)

    def attend_finish(i):
        copy = dkv_copy(i)
        copy.wait()
        there = i * 2 * ITER
        dk = dkv[i % 2, :, 0:ITER] + kv_other[0, :, pl.ds(there, ITER)].astype(F32)
        dv = dkv[i % 2, :, ITER : 2 * ITER] + kv_other[0, :, pl.ds(there + ITER, ITER)].astype(F32)
        hidden[:, pl.ds(i * block + ITER, ITER)] = rotate(dk, -1.0).astype(BF)
        hidden[:, pl.ds(i * block + 2 * ITER, ITER)] = dv.astype(BF)
        here = pl.ds(i * block, block)
        x1[...] += dot(hidden[:, here], mix[:, here], 1, 1)
        made = dot(a_in[...], hidden[:, here], 0, 0)
        store_units(jobs[f"mix{i}a"], 0, made[:, : 2 * ITER])
        store_units(jobs[f"mix{i}b"], 0, made[:, 2 * ITER :])
        job_start(f"mix{i}a", 0)
        job_start(f"mix{i}b", 0)

    def attend_step(i, _):
        attend_back(i)
        dkv_copy(i).start()
        for done in range(iters):

            @pl.when(i == done)
            def _():
                point(f"attend{done}")
                if done == 0:
                    spread_pass(0)
                if done > 0:
                    attend_finish(done - 1)
                    point(f"mix{done - 1}")

        return 0

    lax.fori_loop(0, iters, attend_step, 0)
    attend_finish(iters - 1)
    point(f"mix{iters - 1}")

    def last_rows(i, sums):
        at = pl.ds(aligned(i * ROWS_LN, ROWS_LN), ROWS_LN)
        normed, inverse = normalize(x[at, :])
        grad_in = x1[at, :]
        made = gx[at, :] + norm_back(grad_in * (1.0 + piece_of(SCALE_MIX)), normed, inverse)
        gbf[at, :] = made.astype(BF)
        return sums[0] + col_sum(grad_in), sums[1] + col_sum(grad_in * normed)

    sums = lax.fori_loop(0, rows // ROWS_LN, last_rows, (zero, zero))
    share_start(rows_of(gbf), seq_of(igrad_hbm), 3)
    for index, total in zip((SHIFT_MIX, SCALE_MIX), sums):
        mod[1:2, pl.ds(index * width, width)] = total
    point("last")

    spread_start(1, (SHIFT_MIX, SCALE_MIX), None)

    order = list(PLAN["tail"])
    planned = finished | set(order)
    for stage in range(max(len(job.stages) for job in jobs.values())):
        for name, job in jobs.items():
            if stage < len(job.stages) and (name, stage) not in planned:
                order.append((name, stage))
    for n, (name, stage) in enumerate(order):
        job_finish(name, stage)
        if n == 4:
            spread_pass(1)
    spread_end(0)
    spread_end(1)
    wait_bytes(layer_hbm, share_recv.at[2])
    share_sent(rows_of(x16), seq_of(layer_hbm), 2)
    wait_bytes(igrad_hbm, share_recv.at[3])
    share_sent(rows_of(gbf), seq_of(igrad_hbm), 3)


def per_device(sizes, inputs, cotangent, cond_mask, timestep, embed_table, mix_weight,
               project_weight, up_weight, down_weight, cond_weight, cond_bias):
    seq_count, batch_count = sizes
    seqs_here, pos_here, width = inputs.shape
    hidden_width = up_weight.shape[1]
    length = pos_here * seq_count
    rows = seqs_here * pos_here
    code_rows = -(-seqs_here // 8) * 8
    cosine, sine = rotary_constants(length)
    shares = [
        jax.ShapeDtypeStruct((weight.shape[0] // batch_count, weight.shape[1]), BF)
        for weight in (mix_weight, project_weight, up_weight, down_weight)
    ]
    total = batch_count * seqs_here
    lines = [-(-n * (width // 128) // 8) * 8 for n in (5, 2)]
    shells = [
        jax.ShapeDtypeStruct(weight.shape, BF)
        for weight in (down_weight, up_weight, project_weight, mix_weight)
    ]
    landings, sem_count = [], 0
    for name, job in job_list(shells, [None] * 4, sizes).items():
        for stage, shape in enumerate(job.landing_shapes()):
            if not borrows(name, stage):
                landings.append(pltpu.VMEM(shape, BF))
        sem_count += len(job.stages)
    vmem = pl.BlockSpec(memory_space=pltpu.VMEM)
    hbm = pl.BlockSpec(memory_space=pl.ANY)
    wide = (rows, width)
    smem = pl.BlockSpec(memory_space=pltpu.SMEM)
    smalls = 5
    dma = pltpu.SemaphoreType.DMA
    layer, igrad, share_mix, share_project, share_up, share_down, *gall = pl.pallas_call(
        functools.partial(step_kernel, sizes, seqs_here, pos_here),
        name="block_step",
        out_shape=[
            jax.ShapeDtypeStruct(inputs.shape, BF),
            jax.ShapeDtypeStruct(inputs.shape, BF),
            *shares,
            *[jax.ShapeDtypeStruct((total, count, 128), F32) for count in lines],
        ],
        in_specs=[hbm, hbm, smem, smem, hbm, vmem] + [hbm] * 7,
        out_specs=[hbm, hbm] + [vmem] * 4 + [vmem if total <= 32 else hbm] * 2,
        scratch_shapes=[
            pltpu.VMEM(mix_weight.shape, BF),
            pltpu.VMEM(project_weight.shape, BF),
            pltpu.VMEM(up_weight.shape, BF),
            pltpu.VMEM(down_weight.shape, BF),
            pltpu.VMEM((rows, PAIR), F32),
            pltpu.VMEM((rows, PAIR), F32),
            pltpu.VMEM(wide, BF),
            pltpu.VMEM(wide, BF),
            pltpu.VMEM(wide, F32),
            pltpu.VMEM(wide, F32),
            pltpu.VMEM(wide, BF),
            pltpu.VMEM(wide, BF),
            pltpu.VMEM((rows, 2 * width), BF),
            pltpu.VMEM((2, rows, 2 * width), BF),
            pltpu.VMEM(wide, BF),
            pltpu.VMEM(wide, BF),
            pltpu.VMEM(wide, BF),
            pltpu.VMEM((rows, 2 * width), BF),
            pltpu.VMEM((rows, hidden_width), BF),
            pltpu.VMEM(wide, BF),
            pltpu.VMEM(wide, F32),
            pltpu.VMEM(wide, BF),
            pltpu.VMEM((2, rows, 2 * ITER), F32),
            pltpu.VMEM((rows, 128), F32),
            pltpu.VMEM((8, 6 * width), F32),
            pltpu.VMEM((2 * code_rows, width), F32),
            pltpu.VMEM((2 * code_rows, width), F32),
            *[pltpu.VMEM((2 * seq_count, count, 128), F32) for count in lines],
            landings,
            dma((11,)),
            dma((4,)),
            dma((4,)),
            dma((4,)),
            dma((4,)),
            dma((width // ITER,)),
            dma((width // ITER,)),
            dma((smalls,)),
            dma((smalls,)),
            dma((sem_count,)),
            dma((sem_count,)),
        ],
        compiler_params=pltpu.CompilerParams(
            collective_id=0, has_side_effects=True, vmem_limit_bytes=VMEM_BYTES
        ),
    )(
        inputs,
        cotangent,
        cond_mask,
        timestep,
        embed_table,
        cond_bias.reshape(6 * width // 128, 128),
        jnp.asarray(cosine),
        jnp.asarray(sine),
        mix_weight,
        project_weight,
        up_weight,
        down_weight,
        cond_weight,
    )
    return finish(layer, igrad, share_mix, share_project, share_up, share_down, gall, batch_count)


def finish_kernel(
    batch_count,
    layer_in,
    igrad_in,
    mix_in,
    project_in,
    up_in,
    down_in,
    early_in,
    late_in,
    layer,
    igrad,
    mix,
    project,
    up,
    down,
    cond,
    bias,
    igrad16,
    igrad32,
    early,
    late,
    cond_here,
    layer16,
    project_here,
    up_here,
    down_here,
    mix_here,
    project32,
    up32,
    down32,
    mix32,
    sem,
):
    width = igrad.shape[-1]
    copies = [
        pltpu.make_async_copy(early_in, early, sem.at[sem.shape[0] - 1]),
        pltpu.make_async_copy(late_in, late, sem.at[0]),
    ]
    parts = igrad16.shape[0]
    height = igrad16.shape[1]
    view = [divmod(n * height, igrad.shape[1]) for n in range(parts)]
    loads = [
        pltpu.make_async_copy(
            igrad_in.at[j, pl.ds(row, height), :], igrad16.at[n], sem.at[1 + n]
        )
        for n, (j, row) in enumerate(view)
    ]
    for copy in copies + loads:
        copy.start()
    k = 1 + parts
    moves = [
        (layer_in, layer16, layer16, layer),
        (project_in, project_here, project32, project),
        (up_in, up_here, up32, up),
        (down_in, down_here, down32, down),
        (mix_in, mix_here, mix32, mix),
    ]
    moves_in = [
        pltpu.make_async_copy(source, here, sem.at[k + n])
        for n, (source, here, _, _) in enumerate(moves)
    ]
    for copy in moves_in:
        copy.start()
    k += len(moves)
    outs = []
    for n, (j, row) in enumerate(view):
        loads[n].wait()
        igrad32[n] = igrad16[n].astype(F32)
        outs.append(
            pltpu.make_async_copy(
                igrad32.at[n], igrad.at[j, pl.ds(row, height), :], sem.at[k + n]
            )
        )
        outs[-1].start()
    k += parts
    for n, (_, narrow, here, target) in enumerate(moves):
        moves_in[n].wait()
        if n > 0:
            here[...] = narrow[...].astype(F32)
        pieces = [(here, target)]
        if n == len(moves) - 1:
            pieces = [
                (
                    here.at[:, pl.ds((3 * i + part) * ITER, ITER)],
                    target.at[:, pl.ds(part * width + i * ITER, ITER)],
                )
                for i in range(width // ITER)
                for part in range(3)
            ]
        for here, target in pieces:
            outs.append(pltpu.make_async_copy(here, target, sem.at[k]))
            outs[-1].start()
            k += 1
    for copy in copies:
        copy.wait()
    b = lax.axis_index("batch")
    strips = width // 128
    codes = jnp.concatenate([early[:, n, :] for n in range(4 * strips, 5 * strips)], axis=1)
    grads = jnp.concatenate(
        [late[:, n, :] for n in range(2 * strips)] + [early[:, n, :] for n in range(4 * strips)],
        axis=1,
    )
    mine = width // batch_count
    codes = pltpu.roll(codes, lax.rem(width - b * mine, width), 1)[:, :mine]
    cond_here[...] = lax.dot_general(
        codes,
        grads,
        (((0,), (0,)), ((), ())),
        precision=lax.Precision.HIGHEST,
        preferred_element_type=F32,
    )
    outs.append(pltpu.make_async_copy(cond_here, cond, sem.at[k]))
    outs[-1].start()
    mine = 6 * width // batch_count
    total = jnp.broadcast_to(col_sum(grads), (8, 6 * width))
    total = pltpu.roll(total, lax.rem(6 * width - b * mine, 6 * width), 1)
    bias[...] = total[0, :mine]
    for copy in outs:
        copy.wait()


def finish(layer, igrad, mix, project, up, down, gall, batch_count):
    width = layer.shape[-1]
    vmem = pl.BlockSpec(memory_space=pltpu.VMEM)
    hbm = pl.BlockSpec(memory_space=pl.ANY)
    rows = layer.shape[0] * layer.shape[1]
    parts = 4
    shape = jax.ShapeDtypeStruct
    outs = pl.pallas_call(
        functools.partial(finish_kernel, batch_count),
        name="finish",
        out_shape=[
            shape(layer.shape, BF),
            shape(igrad.shape, F32),
            shape(mix.shape, F32),
            shape(project.shape, F32),
            shape(up.shape, F32),
            shape(down.shape, F32),
            shape((width // batch_count, 6 * width), F32),
            shape((6 * width // batch_count,), F32),
        ],
        in_specs=[hbm] * 8,
        out_specs=[hbm] * 7 + [vmem],
        scratch_shapes=[
            pltpu.VMEM((parts, rows // parts, width), BF),
            pltpu.VMEM((parts, rows // parts, width), F32),
            *[pltpu.VMEM(part.shape, F32) for part in gall],
            pltpu.VMEM((width // batch_count, 6 * width), F32),
            pltpu.VMEM(layer.shape, BF),
            *[pltpu.VMEM(share.shape, BF) for share in (project, up, down, mix)],
            *[pltpu.VMEM(share.shape, F32) for share in (project, up, down, mix)],
            pltpu.SemaphoreType.DMA((12 + 2 * parts + 3 * (width // ITER),)),
        ],
        compiler_params=pltpu.CompilerParams(vmem_limit_bytes=VMEM_BYTES),
    )(layer, igrad, mix, project, up, down, *gall)
    return tuple(outs)


VMEM_BYTES = 64 * 1024 * 1024 - 512 * 1024


def solution(mesh):
    sizes = (mesh.shape["seq"], mesh.shape["batch"])
    split = P("batch", "seq", None)
    placed = (split, split, P("batch"), P("batch")) + (P(),) * 7
    return jax.shard_map(
        functools.partial(per_device, sizes),
        mesh=mesh,
        in_specs=placed,
        out_specs=(split, split) + (P("batch", None),) * 5 + (P("batch"),),
        check_vma=False,
    )
```

```python
import functools
import math

import jax
import jax.numpy as jnp
import numpy as np
from jax import lax
from jax.experimental import pallas as pl
from jax.experimental.pallas import tpu as pltpu
from jax.sharding import PartitionSpec as P

HEAD = 64
PAIR = 2 * HEAD
ITER = 2 * PAIR
EPS = 1e-06
THETA = 10000.0
LOG2E = 1.4426950408889634
SCALE = HEAD ** (-0.5)
EXP_SCALE = SCALE * LOG2E
GELU_A = math.sqrt(2.0 / math.pi)
GELU_B = 0.044715
BF = jnp.bfloat16
F32 = jnp.float32
MESH = pl.DeviceIdType.MESH
ROWS_LN = 256


def dot(left, right, left_dim=1, right_dim=0):
    return lax.dot_general(
        left, right, (((left_dim,), (right_dim,)), ((), ())), preferred_element_type=F32
    )


def lanes(shape):
    return lax.broadcasted_iota(jnp.int32, shape, len(shape) - 1)


def in_head(shape, head):
    return lanes(shape) >= HEAD if head else lanes(shape) < HEAD


def one_head(values, head):
    return jnp.where(in_head(values.shape, head), values, jnp.zeros_like(values))


def bit_of(value, bit):
    return lax.rem(value // bit, 2)


def flip(value, bit):
    return value + bit - 2 * bit * bit_of(value, bit)


def aligned(value, unit):
    return pl.multiple_of(value, unit)


def rotary_constants(length):
    half_size = HEAD // 2
    freqs = THETA ** (-np.arange(half_size, dtype=np.float64) * 2.0 / HEAD)
    angles = np.arange(length, dtype=np.float64)[:, None] * freqs[None, :]
    cosine, sine = np.cos(angles), np.sin(angles)
    cosine = np.concatenate([cosine] * 4, axis=1).astype(np.float32)
    sine = np.concatenate([-sine, sine] * 2, axis=1).astype(np.float32)
    return cosine, sine


def swap_halves(values):
    first = lax.rem(lanes(values.shape), HEAD) < HEAD // 2
    return jnp.where(
        first, pltpu.roll(values, PAIR - HEAD // 2, 1), pltpu.roll(values, HEAD // 2, 1)
    )


def normalize(values):
    row_mean = jnp.mean(values, axis=-1, keepdims=True)
    centered = values - row_mean
    row_var = jnp.mean(centered * centered, axis=-1, keepdims=True)
    inverse = lax.rsqrt(row_var + EPS)
    return centered * inverse, inverse


def norm_back(grad_normed, normed, inverse):
    grad_mean = jnp.mean(grad_normed, axis=-1, keepdims=True)
    cross_mean = jnp.mean(grad_normed * normed, axis=-1, keepdims=True)
    return inverse * (grad_normed - grad_mean - normed * cross_mean)


def col_sum(values):
    return jnp.sum(values, axis=0, keepdims=True)


def bits_of(count):
    return [1 << k for k in range(count.bit_length() - 1)]


def wait_bytes(ref, sem):
    pltpu.make_async_copy(ref, ref, sem).wait()


class Job:
    def __init__(self, grad, out, first, width, kind, sizes):
        self.grad, self.out, self.first, self.width = grad, out, first, width
        self.seq_count, self.batch_count = sizes
        self.row_block = grad.shape[0] // self.batch_count
        self.fold = 1
        while self.row_block * self.fold % 16:
            self.fold *= 2
        self.unit = self.row_block * self.fold
        self.units = self.batch_count // self.fold
        self.order = bits_of(self.units)
        halvings = [("batch", bit) for bit in self.order]
        if kind == "X" and self.fold == 1 and (width // self.seq_count) % PAIR == 0:
            self.stages = (
                halvings[:1]
                + [("cut", bit) for bit in bits_of(self.seq_count)]
                + halvings[1:]
                + [("gather", bit) for bit in bits_of(self.seq_count)[::-1]]
            )
        else:
            self.stages = (
                halvings
                + [("add", bit) for bit in bits_of(self.seq_count)]
                + [("fold", bit) for bit in bits_of(self.fold)]
            )

    def landing_shapes(self):
        count, width, shapes = self.units, self.width, []
        for kind, _ in self.stages:
            if kind == "batch":
                count //= 2
            elif kind == "cut":
                width //= 2
            shapes.append((count * self.unit, width))
            if kind == "gather":
                width *= 2
        return shapes


KINDS = {
    "up0": "Y",
    "up1": "X",
    "up2": "X",
    "up3": "Y",
    "down0": "Y",
    "down1": "X",
    "down2": "Y",
    "project": "X",
    "mix0a": "X",
    "mix0b": "Y",
    "mix1a": "X",
    "mix1b": "Y",
    "mix2a": "Y",
    "mix2b": "Y",
}


def job_list(grads, outs, sizes):
    grad_down, grad_up, grad_project, grad_mix = grads
    out_down, out_up, out_project, out_mix = outs
    model_width, hidden_width = grad_up.shape
    jobs = {}

    def add(name, grad, out, first, width):
        jobs[name] = Job(grad, out, first, width, KINDS[name], sizes)

    for i in range(hidden_width // model_width):
        add(f"up{i}", grad_up, out_up, i * model_width, model_width)
    for i in range(model_width // ITER):
        add(f"down{i}", grad_down, out_down, i * ITER, ITER)
    add("project", grad_project, out_project, 0, model_width)
    for i in range(model_width // ITER):
        add(f"mix{i}a", grad_mix, out_mix, i * 3 * ITER, 2 * ITER)
        add(f"mix{i}b", grad_mix, out_mix, i * 3 * ITER + 2 * ITER, ITER)
    return jobs


def borrows(name, stage):
    return name.startswith("mix") and stage == 0


PLAN = {
    "up0": (),
    "up1": (
        ("up0", 0),
    ),
    "up2": (
        ("up1", 0),
    ),
    "up3": (
        ("up2", 0),
    ),
    "feed": (
        ("up0", 1), ("up3", 0),
    ),
    "down": (
        ("up1", 1),
    ),
    "middle": (),
    "project": (
        ("up0", 2), ("down0", 0),
    ),
    "attend0": (
        ("up2", 1), ("down1", 0), ("up3", 1), ("down2", 0), ("up1", 2),
        ("project", 0), ("up0", 3),
    ),
    "attend1": (
        ("up3", 2), ("down0", 1),
    ),
    "mix0": (
        ("up1", 3), ("up2", 2),
    ),
    "attend2": (
        ("down1", 1), ("mix0a", 0), ("mix0b", 0), ("up3", 3), ("down0", 2),
        ("up1", 4),
    ),
    "mix1": (
        ("up2", 3), ("project", 1), ("down2", 1), ("up0", 4),
    ),
    "mix2": (
        ("mix1a", 0), ("down1", 2), ("mix1b", 0), ("mix0a", 1), ("down0", 3),
        ("mix0b", 1), ("up3", 4), ("up2", 4), ("up1", 5), ("down2", 2),
        ("mix2a", 0), ("project", 2), ("mix2b", 0),
    ),
    "last": (),
    "tail": (
        ("down1", 3), ("mix1b", 1), ("mix0b", 2), ("mix1a", 1), ("mix0a", 2),
        ("down0", 4), ("down2", 3), ("project", 3), ("up2", 5), ("mix2a", 1),
        ("down1", 4), ("mix1b", 2), ("mix0b", 3), ("mix0a", 3), ("mix2b", 1),
        ("project", 4), ("mix1a", 2), ("mix2a", 2), ("mix1b", 3), ("mix0a", 4),
        ("mix2b", 2), ("mix1a", 3), ("down2", 4), ("mix2a", 3), ("down1", 5),
        ("mix0b", 4), ("mix2b", 3), ("project", 5), ("mix1b", 4), ("mix1a", 4),
        ("mix0a", 5), ("mix2a", 4), ("mix2b", 4), ("mix1a", 5),
    ),
}


def step_kernel(
    sizes,
    seqs_here,
    pos_here,
    inputs_hbm,
    cot_hbm,
    flags_ref,
    steps_ref,
    table_hbm,
    bias_ref,
    cos_hbm,
    sin_hbm,
    mix_hbm,
    project_hbm,
    up_hbm,
    down_hbm,
    cond_hbm,
    layer_hbm,
    igrad_hbm,
    out_mix,
    out_project,
    out_up,
    out_down,
    out_early,
    out_late,
    mix,
    project,
    up,
    down,
    cos,
    sin,
    x16,
    cot,
    x,
    x1,
    a_in,
    q,
    kv,
    kv_other,
    mixed,
    branch,
    b_in,
    dkv_out,
    hidden,
    gbf,
    gx,
    dout,
    dkv,
    lse,
    mod,
    codes,
    codes_other,
    sums_early,
    sums_late,
    landings,
    load_sem,
    share_sem,
    share_recv,
    kv_sem,
    kv_recv,
    dkv_sem,
    dkv_recv,
    small_sem,
    small_recv,
    job_sem,
    job_recv,
):
    seq_count, batch_count = sizes
    out_all, sums_here = (out_early, out_late), (sums_early, sums_late)
    rows, width = x.shape
    hidden_width = up.shape[1]
    pairs = width // PAIR
    iters = width // ITER
    block = 3 * ITER
    s = lax.axis_index("seq")
    b = lax.axis_index("batch")
    core = lax.rem(b, 2)
    core_peer = (s, flip(b, 1))

    barrier = pltpu.get_barrier_semaphore()
    chip_count = batch_count // 2
    chip = b // 2
    near = [
        (lax.rem(s + n // 2, seq_count), flip(b, 1) if n % 2 else b)
        for n in range(1, 2 * seq_count)
    ]
    far = [(s, 2 * lax.rem(chip + n, chip_count) + core) for n in range(1, chip_count)]
    peers = near + far
    for peer in peers:
        pl.semaphore_signal(barrier, inc=1, device_id=peer, device_id_type=MESH)

    def share_peer(j):
        return core * seqs_here + j, b - core + s // seqs_here

    def is_self(j):
        ps, pb = share_peer(j)
        return jnp.logical_and(ps == s, pb == b)

    for j in range(seqs_here):

        @pl.when(jnp.logical_not(is_self(j)))
        def _():
            pl.semaphore_signal(barrier, inc=1, device_id=share_peer(j), device_id_type=MESH)

    own = jnp.where(s // seqs_here == core, 1, 0)

    table_size = table_hbm.shape[0]
    table_loads = []
    for n, target in enumerate((x, x1)):
        count = min(rows, table_size - n * rows)
        table_loads.append(
            pltpu.make_async_copy(
                table_hbm.at[pl.ds(n * rows, count), :],
                target.at[pl.ds(0, count), :],
                load_sem.at[9 + n],
            )
        )
        table_loads[-1].start()
    cond_up = pltpu.make_async_copy(cond_hbm.at[:, pl.ds(0, hidden_width)], up, load_sem.at[0])
    cond_up.start()
    rest = cond_hbm.shape[1] - hidden_width
    cond_down = []
    for i in range(rest // width):
        cond_down.append(
            pltpu.make_async_copy(
                cond_hbm.at[:, pl.ds(hidden_width + i * width, width)],
                down.at[pl.ds(i * width, width), :],
                load_sem.at[1 + i],
            )
        )
        cond_down[-1].start()
    mix_loads = []
    for i in range(iters):
        for part in range(3):
            mix_loads.append(
                pltpu.make_async_copy(
                    mix_hbm.at[:, pl.ds(part * width + i * ITER, ITER)],
                    mix.at[:, pl.ds(i * block + part * ITER, ITER)],
                    load_sem.at[8],
                )
            )
            mix_loads[-1].start()
    row0 = core * rows
    load_cos = pltpu.make_async_copy(
        cos_hbm.at[pl.ds(aligned(row0, 128), rows), :], cos, load_sem.at[5]
    )
    load_sin = pltpu.make_async_copy(
        sin_hbm.at[pl.ds(aligned(row0, 128), rows), :], sin, load_sem.at[6]
    )
    load_project = pltpu.make_async_copy(project_hbm, project, load_sem.at[7])
    load_cos.start()
    load_sin.start()
    load_project.start()

    pl.semaphore_wait(barrier, len(peers) + seqs_here - own)

    def share_copy(source, target, j, k):
        return pltpu.make_async_remote_copy(
            src_ref=source,
            dst_ref=target,
            send_sem=share_sem.at[k],
            recv_sem=share_recv.at[k],
            device_id=share_peer(j),
            device_id_type=MESH,
        )

    slot = lax.rem(s, seqs_here)

    def share_start(source, target, k):
        for j in range(seqs_here):

            @pl.when(is_self(j))
            def _():
                pltpu.make_async_copy(source(j), target(slot), share_recv.at[k]).start()

            @pl.when(jnp.logical_not(is_self(j)))
            def _():
                share_copy(source(j), target(slot), j, k).start()

    def share_sent(source, target, k):
        for j in range(seqs_here):

            @pl.when(jnp.logical_not(is_self(j)))
            def _():
                share_copy(source(j), target(slot), j, k).wait_send()

    def rows_of(ref):
        return lambda j: ref.at[pl.ds(aligned(j * pos_here, 16), pos_here), :]

    def seq_of(ref):
        return lambda j: ref.at[j]

    def to_core(source, target, sems, recvs, k):
        return pltpu.make_async_remote_copy(
            src_ref=source,
            dst_ref=target,
            send_sem=sems.at[k],
            recv_sem=recvs.at[k],
            device_id=core_peer,
            device_id_type=MESH,
        )

    share_start(seq_of(inputs_hbm), rows_of(x16), 0)
    for load in table_loads:
        load.wait()
    half_rows = codes.shape[0] // 2
    codes[...] = jnp.zeros_like(codes)
    for j in range(seqs_here):
        time = steps_ref[j]
        low = x[pl.ds(jnp.minimum(time, rows - 1), 1), :]
        high = x1[pl.ds(jnp.maximum(time - rows, 0), 1), :]
        embedding = jnp.where(time < rows, low, high)
        codes[j : j + 1, :] = jax.nn.silu(embedding).astype(BF).astype(F32)
        codes[half_rows + j : half_rows + j + 1, :] = jnp.full(
            (1, width), flags_ref[j].astype(F32)
        )
    code_copy = to_core(codes, codes_other, small_sem, small_recv, 0)
    code_copy.start()

    code_copy.wait()
    own_f = own.astype(F32)
    code_rows = codes[...] * own_f + codes_other[...] * (1.0 - own_f)
    row_ids = lax.broadcasted_iota(jnp.int32, code_rows.shape, 0)
    code = col_sum(jnp.where(row_ids == slot, code_rows, 0.0))
    flag = col_sum(jnp.where(row_ids == slot + half_rows, code_rows, 0.0))
    code_lhs = jnp.broadcast_to(code, (8, width)).astype(BF)
    strips = width // 128

    def bias_of(piece):
        return jnp.concatenate(
            [bias_ref[piece * strips + n : piece * strips + n + 1, :] for n in range(strips)], axis=1
        )

    cond_up.wait()
    for piece in range(hidden_width // width):
        at = slice(piece * width, (piece + 1) * width)
        mod[:, at] = dot(code_lhs, up[:, at]) + bias_of(piece)
    load_up = pltpu.make_async_copy(up_hbm, up, load_sem.at[0])
    load_up.start()
    for i in range(rest // width):
        cond_down[i].wait()
        at = slice(hidden_width + i * width, hidden_width + (i + 1) * width)
        mod[:, at] = dot(code_lhs, down[i * width : (i + 1) * width, :]) + bias_of(
            hidden_width // width + i
        )
    load_down = pltpu.make_async_copy(down_hbm, down, load_sem.at[1])
    load_down.start()

    def piece_of(index, start=0, size=None):
        size = width if size is None else size
        return mod[0:1, pl.ds(index * width + start, size)]

    SHIFT_MIX, SCALE_MIX, GATE_MIX, SHIFT_FEED, SCALE_FEED, GATE_FEED = range(6)

    def norm_rows(source, target, shift_index, scale_index):
        def body(i, _):
            at = pl.ds(aligned(i * ROWS_LN, ROWS_LN), ROWS_LN)
            normed, _ = normalize(source[at, :].astype(F32))
            target[at, :] = (
                normed * (1.0 + piece_of(scale_index)) + piece_of(shift_index)
            ).astype(BF)
            return 0

        lax.fori_loop(0, rows // ROWS_LN, body, 0)

    def rotate(values, sign):
        parts = []
        for p in range(values.shape[1] // PAIR):
            part = values[:, p * PAIR : (p + 1) * PAIR]
            parts.append(part * cos[...] + sign * (swap_halves(part) * sin[...]))
        return jnp.concatenate(parts, axis=1)

    def project_part(part, target, base):
        def body(i, _):
            made = dot(a_in[...], mix[:, pl.ds(aligned(i * block + part * ITER, ITER), ITER)])
            if part < 2:
                made = rotate(made, 1.0)
            target[:, pl.ds(aligned(base + i * ITER, ITER), ITER)] = made.astype(BF)
            return 0

        lax.fori_loop(0, iters, body, 0, unroll=True)

    def kv_copy(which, part):
        at = pl.ds(part * width, width)
        return to_core(kv.at[:, at], kv_other.at[which, :, at], kv_sem, kv_recv, 2 * which + part)

    def attend(which):
        group = pairs // 2

        def body(i, _):
            for inner in range(group):
                pair = i * group + inner
                at = pl.ds(aligned(pair * PAIR, PAIR), PAIR)
                at_v = pl.ds(aligned(width + pair * PAIR, PAIR), PAIR)
                query = q[:, at]
                key = jnp.concatenate([kv[:, at], kv_other[which, :, at]], axis=0)
                value = jnp.concatenate([kv[:, at_v], kv_other[which, :, at_v]], axis=0)
                outs = []
                for head in range(2):
                    scores = dot(one_head(query, head), key, 1, 1)
                    top = jnp.max(scores, axis=1, keepdims=True)
                    weights = jnp.exp2((scores - top) * EXP_SCALE)
                    ones = jnp.where(in_head(value.shape, head), value, jnp.ones_like(value))
                    made = dot(weights.astype(BF), ones)
                    total = made[:, HEAD * (1 - head) : HEAD * (1 - head) + 1]
                    outs.append(made * (1.0 / total))
                    level = top * EXP_SCALE + jnp.log2(total)
                    lse[...] = jnp.where(lanes(lse.shape) == 2 * pair + head, level, lse[...])
                mixed[:, at] = jnp.where(
                    lanes(outs[0].shape) < HEAD, outs[0], outs[1]
                ).astype(BF)
            return 0

        lax.fori_loop(0, 2, body, 0)

    wait_bytes(x16, share_recv.at[0])
    share_start(seq_of(cot_hbm), rows_of(cot), 1)
    for load in mix_loads + [load_cos, load_sin, load_project, load_up, load_down]:
        load.wait()
    x[...] = x16[...].astype(F32)

    def forward(which, _):
        norm_rows(x, a_in, SHIFT_MIX, SCALE_MIX)
        project_part(1, kv, 0)
        key_copy = kv_copy(which, 0)
        key_copy.start()
        project_part(2, kv, width)
        value_copy = kv_copy(which, 1)
        value_copy.start()
        project_part(0, q, 0)
        key_copy.wait()
        value_copy.wait()
        attend(which)

        def mix_out(i, _):
            at = pl.ds(aligned(i * ITER, ITER), ITER)
            made = dot(mixed[...], project[:, at])
            branch[:, at] = made.astype(BF)
            gate = mod[0:1, pl.ds(aligned(GATE_MIX * width + i * ITER, ITER), ITER)]
            x1[:, at] = x[:, at] + gate * made
            return 0

        lax.fori_loop(0, iters, mix_out, 0, unroll=True)
        norm_rows(x1, b_in, SHIFT_FEED, SCALE_FEED)

        @pl.when(which == 0)
        def _():
            step = 2 * ITER

            def feed_up(i, _):
                at = pl.ds(aligned(i * step, step), step)
                pre = dot(b_in[...], up[:, at])
                inner = jnp.tanh(pre * (GELU_A + (GELU_A * GELU_B) * (pre * pre)))
                hidden[:, at] = (pre * (0.5 * (1.0 + inner))).astype(BF)
                return 0

            lax.fori_loop(0, hidden_width // step, feed_up, 0, unroll=2)

            def feed_down(i, _):
                at = pl.ds(aligned(i * ITER, ITER), ITER)
                gate = mod[0:1, pl.ds(aligned(GATE_FEED * width + i * ITER, ITER), ITER)]
                result = x1[:, at] + gate * dot(hidden[...], down[:, at])
                x[:, at] = x[:, at] + flag[:, 0:1] * result
                return 0

            lax.fori_loop(0, iters, feed_down, 0)

        return 0

    lax.fori_loop(0, 2, forward, 0)
    share_sent(seq_of(inputs_hbm), rows_of(x16), 0)
    wait_bytes(cot, share_recv.at[1])
    share_sent(seq_of(cot_hbm), rows_of(cot), 1)

    jobs = job_list((down, up, project, mix), (out_down, out_up, out_project, out_mix), sizes)
    spare, sem_at = list(landings), 0
    for name, job in jobs.items():
        job.landing = []
        for stage in range(len(job.stages)):
            if borrows(name, stage):
                lender = jobs["up" + name[3]].landing[0]
                job.landing.append(lender.at[:, pl.ds(job.first % block, job.width)])
            else:
                job.landing.append(spare.pop(0))
        job.sem_base = sem_at
        sem_at += len(job.stages)

    def job_view(job, stage):
        me = b // job.fold
        row, height, start, wide = 0, job.units * job.unit, job.first, job.width
        for kind, bit in job.stages[:stage]:
            if kind == "batch":
                height //= 2
                row = row + bit_of(me, bit) * height
            elif kind == "cut":
                wide //= 2
                start = start + bit_of(s, bit) * wide
        return row, height, start, wide

    def gather_view(job, stage):
        start, wide = job.first, job.width
        done = [bit for kind, bit in job.stages[:stage] if kind == "gather"]
        for kind, bit in job.stages:
            if kind == "cut" and bit not in done:
                wide //= 2
                start = start + bit_of(s, bit) * wide
        return start, wide

    def job_copy(job, stage):
        kind, bit = job.stages[stage]
        row, height, start, wide = job_view(job, stage)
        peer = (flip(s, bit), b)
        if kind == "batch":
            height //= 2
            row = row + (1 - bit_of(b // job.fold, bit)) * height
            peer = (s, flip(b, bit * job.fold))
        elif kind == "cut":
            wide //= 2
            start = start + (1 - bit_of(s, bit)) * wide
        elif kind == "gather":
            start, wide = gather_view(job, stage)
        elif kind == "fold":
            peer = (s, flip(b, bit))
        return pltpu.make_async_remote_copy(
            src_ref=job.grad.at[
                pl.ds(aligned(row, job.unit), height), pl.ds(aligned(start, PAIR), wide)
            ],
            dst_ref=job.landing[stage],
            send_sem=job_sem.at[job.sem_base + stage],
            recv_sem=job_recv.at[job.sem_base + stage],
            device_id=peer,
            device_id_type=MESH,
        )

    def job_start(name, stage):
        job_copy(jobs[name], stage).start()

    def job_finish(name, stage):
        job = jobs[name]
        kind, bit = job.stages[stage]
        land = job.landing[stage]
        job_copy(job, stage).wait()
        last = stage == len(job.stages) - 1
        row, height, start, wide = job_view(job, stage + 1)
        at = pl.ds(aligned(row, job.unit), height)
        cols = pl.ds(aligned(start, PAIR), wide)
        if kind in ("batch", "cut"):

            def body(t, _):
                here = pl.ds(aligned(row + t * job.unit, job.unit), job.unit)
                there = pl.ds(aligned(t * job.unit, job.unit), job.unit)
                job.grad[here, cols] = job.grad[here, cols] + land[there, :]
                return 0

            lax.fori_loop(0, height // job.unit, body, 0)
        elif kind in ("add", "fold"):
            total = job.grad[at, cols].astype(F32) + land[...].astype(F32)
            if last:
                mine = total[: job.row_block]
                for n in range(1, job.fold):
                    here = total[n * job.row_block : (n + 1) * job.row_block]
                    mine = jnp.where(lax.rem(b, job.fold) == n, here, mine)
                job.out[:, cols] = mine.astype(BF)
            else:
                job.grad[at, cols] = total.astype(BF)
        else:
            start, wide = gather_view(job, stage)
            cols = pl.ds(aligned(start, PAIR), wide)
            theirs = pl.ds(aligned(start + (1 - 2 * bit_of(s, bit)) * wide, PAIR), wide)
            if last:
                job.out[:, cols] = job.grad[at, cols]
                job.out[:, theirs] = land[...]
            else:
                job.grad[at, theirs] = land[...]
        if not last:
            job_start(name, stage + 1)

    def spread_near(k):
        place = 2 * s + core
        return [
            pltpu.make_async_remote_copy(
                src_ref=sums_here[k].at[place],
                dst_ref=sums_here[k].at[place],
                send_sem=small_sem.at[2 * k + 1],
                recv_sem=small_recv.at[2 * k + 1],
                device_id=peer,
                device_id_type=MESH,
            )
            for peer in near
        ]

    def spread_far(k):
        here = out_all[k].at[pl.ds(chip * seq_count, seq_count)]
        return [
            pltpu.make_async_remote_copy(
                src_ref=here,
                dst_ref=here,
                send_sem=small_sem.at[2 * k + 2],
                recv_sem=small_recv.at[2 * k + 2],
                device_id=peer,
                device_id_type=MESH,
            )
            for peer in far
        ]

    def spread_start(k, pieces, tail):
        place = 2 * s + core
        line = 0
        for index in pieces:
            for strip in range(strips):
                at = slice(index * width + strip * 128, index * width + (strip + 1) * 128)
                sums_here[k][place, line : line + 1, :] = mod[1:2, at]
                line += 1
        if tail is not None:
            for strip in range(strips):
                sums_here[k][place, line : line + 1, :] = 0.5 * tail[
                    :, strip * 128 : (strip + 1) * 128
                ]
                line += 1
        left = sums_here[k].shape[1] - line
        if left:
            sums_here[k][place, line:, :] = jnp.zeros((left, 128), F32)
        for copy in spread_near(k):
            copy.start()

    def spread_pass(k):
        count = 2 * seq_count - 1
        wait_bytes(sums_here[k].at[pl.ds(0, count)], small_recv.at[2 * k + 1])
        wait_bytes(sums_here[k].at[pl.ds(0, count)], small_sem.at[2 * k + 1])
        for n in range(seq_count):
            sums_here[k][2 * n] = sums_here[k][2 * n] + sums_here[k][2 * n + 1]
            keep = pltpu.make_async_copy(
                sums_here[k].at[2 * n], out_all[k].at[chip * seq_count + n], load_sem.at[9 + n % 2]
            )
            keep.start()
            keep.wait()
        for copy in spread_far(k):
            copy.start()

    def spread_end(k):
        count = (chip_count - 1) * seq_count
        wait_bytes(out_all[k].at[pl.ds(0, count)], small_recv.at[2 * k + 2])
        wait_bytes(out_all[k].at[pl.ds(0, count)], small_sem.at[2 * k + 2])

    finished = set()

    def point(name):
        for entry in PLAN[name]:
            job_finish(*entry)
            finished.add(entry)

    def store_units(job, cols, first, made):
        for n in range(made.shape[0] // job.unit):
            place = 0
            for bit in job.order:
                place = 2 * place + (first + n) // bit % 2
            job.grad[pl.ds(aligned(place * job.unit, job.unit), job.unit), cols] = made[
                n * job.unit : (n + 1) * job.unit
            ].astype(BF)

    for i in range(iters):
        at = slice(i * ITER, (i + 1) * ITER)
        gate = piece_of(GATE_FEED, i * ITER, ITER)
        gbf[:, at] = (gate * cot[:, at].astype(F32)).astype(BF)
    gx[...] = jnp.zeros_like(gx)

    def feed_back(i, _):
        at = pl.ds(aligned(i * width, width), width)
        pre = dot(b_in[...], up[:, at])
        square = pre * pre
        inner = jnp.tanh(pre * (GELU_A + (GELU_A * GELU_B) * square))
        left = 0.5 * (1.0 + inner)
        hidden[:, at] = (pre * left).astype(BF)
        bend = GELU_A + (3.0 * GELU_A * GELU_B) * square
        slope = left + (0.5 * pre) * (1.0 - inner * inner) * bend
        grad_pre = (dot(gbf[...], down[at, :], 1, 1) * slope).astype(BF)
        gx[...] += dot(grad_pre, up[:, at], 1, 1)
        store_units(jobs["up0"], at, 0, dot(b_in[...], grad_pre, 0, 0))
        for n in range(hidden_width // width):

            @pl.when(i == n)
            def _():
                job_start(f"up{n}", 0)
                if n > 0:
                    point(f"up{n}")

        return 0

    lax.fori_loop(0, hidden_width // width, feed_back, 0)

    def feed_out(i, _):
        at = pl.ds(aligned(i * ITER, ITER), ITER)
        made = dot(hidden[...], down[:, at])
        gate_at = pl.ds(aligned(GATE_FEED * width + i * ITER, ITER), ITER)
        x16[:, at] = (x1[:, at] + mod[0:1, gate_at] * made).astype(BF)
        mod[1:2, gate_at] = col_sum(cot[:, at].astype(F32) * made)
        return 0

    lax.fori_loop(0, iters, feed_out, 0)
    point("feed")

    def feed_down_grad(i, _):
        at = pl.ds(aligned(i * width, width), width)
        made = dot(hidden[:, at], gbf[...], 0, 0)
        store_units(jobs["down0"], slice(None), i * (width // jobs["down0"].unit), made)
        return 0

    lax.fori_loop(0, hidden_width // width, feed_down_grad, 0)
    for i in range(iters):
        job_start(f"down{i}", 0)
    share_start(rows_of(x16), seq_of(layer_hbm), 2)
    point("down")

    def middle_rows(i, sums):
        at = pl.ds(aligned(i * ROWS_LN, ROWS_LN), ROWS_LN)
        normed, inverse = normalize(x1[at, :])
        grad_in = gx[at, :]
        made = cot[at, :].astype(F32) + norm_back(
            grad_in * (1.0 + piece_of(SCALE_FEED)), normed, inverse
        )
        gx[at, :] = made
        gbf[at, :] = (piece_of(GATE_MIX) * made).astype(BF)
        return (
            sums[0] + col_sum(grad_in),
            sums[1] + col_sum(grad_in * normed),
            sums[2] + col_sum(made * branch[at, :].astype(F32)),
        )

    zero = jnp.zeros((1, width), F32)
    sums = lax.fori_loop(0, rows // ROWS_LN, middle_rows, (zero, zero, zero))
    for index, total in zip((SHIFT_FEED, SCALE_FEED, GATE_MIX), sums):
        mod[1:2, pl.ds(index * width, width)] = total
    point("middle")

    def project_back(i, _):
        at = pl.ds(aligned(i * ITER, ITER), ITER)
        dout[:, at] = dot(gbf[...], project[at, :], 1, 1).astype(BF)
        return 0

    lax.fori_loop(0, iters, project_back, 0)
    store_units(jobs["project"], slice(None), 0, dot(mixed[...], gbf[...], 0, 0))
    job_start("project", 0)
    spread_start(0, (GATE_MIX, SHIFT_FEED, SCALE_FEED, GATE_FEED), code)
    point("project")
    x1[...] = jnp.zeros_like(x1)

    def dkv_copy(i):
        at = pl.ds(aligned(i * 2 * ITER, 2 * ITER), 2 * ITER)
        return to_core(dkv_out.at[:, at], kv_other.at[0, :, at], dkv_sem, dkv_recv, i)

    def attend_back(i):
        for inner in range(2):
            pair = 2 * i + inner
            at = pl.ds(aligned(pair * PAIR, PAIR), PAIR)
            at_v = pl.ds(aligned(width + pair * PAIR, PAIR), PAIR)
            query, grads = q[:, at], dout[:, at]
            key = jnp.concatenate([kv[:, at], kv_other[1, :, at]], axis=0)
            value = jnp.concatenate([kv[:, at_v], kv_other[1, :, at_v]], axis=0)
            crossed = grads.astype(F32) * mixed[:, at].astype(F32)
            lane_q, lane_k = lanes(query.shape), lanes(key.shape)
            dq = dk = dv = None
            for head in range(2):
                spare = HEAD * (1 - head)
                query_h, grads_h = one_head(query, head), one_head(grads, head)
                key_h = one_head(key, head)
                level = jnp.sum(
                    jnp.where(lanes(lse.shape) == 2 * pair + head, lse[...], 0.0),
                    axis=1,
                    keepdims=True,
                )
                delta = jnp.sum(one_head(crossed, head), axis=1, keepdims=True)
                scaled = query_h.astype(F32) * EXP_SCALE
                high = scaled.astype(BF)
                low = (scaled - high.astype(F32)).astype(BF)
                level1 = (-level).astype(BF)
                left = -level - level1.astype(F32)
                level2 = left.astype(BF)
                level3 = (left - level2.astype(F32)).astype(BF)
                low = jnp.where(lane_q == spare, level1, low)
                low = jnp.where(lane_q == spare + 1, level2, low)
                low = jnp.where(lane_q == spare + 2, level3, low)
                key_low = jnp.where(
                    jnp.logical_and(lane_k >= spare, lane_k < spare + 3),
                    jnp.ones_like(key),
                    key_h,
                )
                probs = jnp.exp2(
                    dot(
                        jnp.concatenate([high, low], axis=1),
                        jnp.concatenate([key_h, key_low], axis=1),
                        1,
                        1,
                    )
                )
                delta1 = (-delta).astype(BF)
                delta2 = (-delta - delta1.astype(F32)).astype(BF)
                grads_d = jnp.where(lane_q == spare, delta1, grads_h)
                grads_d = jnp.where(lane_q == spare + 1, delta2, grads_d)
                value_d = jnp.where(
                    jnp.logical_and(lane_k >= spare, lane_k < spare + 2),
                    jnp.ones_like(value),
                    value,
                )
                grad_scores = (probs * dot(grads_d, value_d, 1, 1)).astype(BF)
                dv_h = dot(grads_h, probs.astype(BF), 0, 0)
                dk_h = dot(query_h, grad_scores, 0, 0)
                dq_h = dot(grad_scores, key_h)
                if head == 0:
                    dq, dk, dv = dq_h, dk_h, dv_h
                else:
                    dq, dk, dv = dq + dq_h, dk + dk_h, dv + dv_h
            hidden[:, pl.ds(aligned(i * block + inner * PAIR, PAIR), PAIR)] = rotate(
                dq * SCALE, -1.0
            ).astype(BF)
            for part, made in ((0, dk.T * SCALE), (1, dv.T)):
                off = part * ITER + inner * PAIR
                dkv[lax.rem(i, 2), :, pl.ds(off, PAIR)] = made[:rows]
                dkv_out[:, pl.ds(aligned(i * 2 * ITER + off, PAIR), PAIR)] = made[rows:].astype(BF)

    def attend_finish(i):
        copy = dkv_copy(i)
        copy.wait()
        there = i * 2 * ITER
        dk = dkv[i % 2, :, 0:ITER] + kv_other[0, :, pl.ds(there, ITER)].astype(F32)
        dv = dkv[i % 2, :, ITER : 2 * ITER] + kv_other[0, :, pl.ds(there + ITER, ITER)].astype(F32)
        hidden[:, pl.ds(i * block + ITER, ITER)] = rotate(dk, -1.0).astype(BF)
        hidden[:, pl.ds(i * block + 2 * ITER, ITER)] = dv.astype(BF)
        here = pl.ds(i * block, block)
        x1[...] += dot(hidden[:, here], mix[:, here], 1, 1)
        store_units(jobs[f"mix{i}a"], here, 0, dot(a_in[...], hidden[:, here], 0, 0))
        job_start(f"mix{i}a", 0)
        job_start(f"mix{i}b", 0)

    def attend_step(i, _):
        attend_back(i)
        dkv_copy(i).start()
        for done in range(iters):

            @pl.when(i == done)
            def _():
                point(f"attend{done}")
                if done == 0:
                    spread_pass(0)
                if done > 0:
                    attend_finish(done - 1)
                    point(f"mix{done - 1}")

        return 0

    lax.fori_loop(0, iters, attend_step, 0)
    attend_finish(iters - 1)
    point(f"mix{iters - 1}")

    def last_rows(i, sums):
        at = pl.ds(aligned(i * ROWS_LN, ROWS_LN), ROWS_LN)
        normed, inverse = normalize(x[at, :])
        grad_in = x1[at, :]
        made = gx[at, :] + norm_back(grad_in * (1.0 + piece_of(SCALE_MIX)), normed, inverse)
        gbf[at, :] = made.astype(BF)
        return sums[0] + col_sum(grad_in), sums[1] + col_sum(grad_in * normed)

    sums = lax.fori_loop(0, rows // ROWS_LN, last_rows, (zero, zero))
    share_start(rows_of(gbf), seq_of(igrad_hbm), 3)
    for index, total in zip((SHIFT_MIX, SCALE_MIX), sums):
        mod[1:2, pl.ds(index * width, width)] = total
    point("last")

    spread_start(1, (SHIFT_MIX, SCALE_MIX), None)

    order = list(PLAN["tail"])
    planned = finished | set(order)
    for stage in range(max(len(job.stages) for job in jobs.values())):
        for name, job in jobs.items():
            if stage < len(job.stages) and (name, stage) not in planned:
                order.append((name, stage))
    for n, (name, stage) in enumerate(order):
        job_finish(name, stage)
        if n == 4:
            spread_pass(1)
    spread_end(0)
    spread_end(1)
    wait_bytes(layer_hbm, share_recv.at[2])
    share_sent(rows_of(x16), seq_of(layer_hbm), 2)
    wait_bytes(igrad_hbm, share_recv.at[3])
    share_sent(rows_of(gbf), seq_of(igrad_hbm), 3)


def per_device(sizes, inputs, cotangent, cond_mask, timestep, embed_table, mix_weight,
               project_weight, up_weight, down_weight, cond_weight, cond_bias):
    seq_count, batch_count = sizes
    seqs_here, pos_here, width = inputs.shape
    hidden_width = up_weight.shape[1]
    length = pos_here * seq_count
    rows = seqs_here * pos_here
    code_rows = -(-seqs_here // 8) * 8
    cosine, sine = rotary_constants(length)
    shares = [
        jax.ShapeDtypeStruct((weight.shape[0] // batch_count, weight.shape[1]), BF)
        for weight in (mix_weight, project_weight, up_weight, down_weight)
    ]
    total = batch_count * seqs_here
    lines = [-(-n * (width // 128) // 8) * 8 for n in (5, 2)]
    shells = [
        jax.ShapeDtypeStruct(weight.shape, BF)
        for weight in (down_weight, up_weight, project_weight, mix_weight)
    ]
    landings, sem_count = [], 0
    for name, job in job_list(shells, [None] * 4, sizes).items():
        for stage, shape in enumerate(job.landing_shapes()):
            if not borrows(name, stage):
                landings.append(pltpu.VMEM(shape, BF))
        sem_count += len(job.stages)
    vmem = pl.BlockSpec(memory_space=pltpu.VMEM)
    hbm = pl.BlockSpec(memory_space=pl.ANY)
    wide = (rows, width)
    smem = pl.BlockSpec(memory_space=pltpu.SMEM)
    smalls = 5
    dma = pltpu.SemaphoreType.DMA
    layer, igrad, share_mix, share_project, share_up, share_down, *gall = pl.pallas_call(
        functools.partial(step_kernel, sizes, seqs_here, pos_here),
        name="block_step",
        out_shape=[
            jax.ShapeDtypeStruct(inputs.shape, BF),
            jax.ShapeDtypeStruct(inputs.shape, BF),
            *shares,
            *[jax.ShapeDtypeStruct((total, count, 128), F32) for count in lines],
        ],
        in_specs=[hbm, hbm, smem, smem, hbm, vmem] + [hbm] * 7,
        out_specs=[hbm, hbm] + [vmem] * 4 + [vmem if total <= 32 else hbm] * 2,
        scratch_shapes=[
            pltpu.VMEM(mix_weight.shape, BF),
            pltpu.VMEM(project_weight.shape, BF),
            pltpu.VMEM(up_weight.shape, BF),
            pltpu.VMEM(down_weight.shape, BF),
            pltpu.VMEM((rows, PAIR), F32),
            pltpu.VMEM((rows, PAIR), F32),
            pltpu.VMEM(wide, BF),
            pltpu.VMEM(wide, BF),
            pltpu.VMEM(wide, F32),
            pltpu.VMEM(wide, F32),
            pltpu.VMEM(wide, BF),
            pltpu.VMEM(wide, BF),
            pltpu.VMEM((rows, 2 * width), BF),
            pltpu.VMEM((2, rows, 2 * width), BF),
            pltpu.VMEM(wide, BF),
            pltpu.VMEM(wide, BF),
            pltpu.VMEM(wide, BF),
            pltpu.VMEM((rows, 2 * width), BF),
            pltpu.VMEM((rows, hidden_width), BF),
            pltpu.VMEM(wide, BF),
            pltpu.VMEM(wide, F32),
            pltpu.VMEM(wide, BF),
            pltpu.VMEM((2, rows, 2 * ITER), F32),
            pltpu.VMEM((rows, 128), F32),
            pltpu.VMEM((8, 6 * width), F32),
            pltpu.VMEM((2 * code_rows, width), F32),
            pltpu.VMEM((2 * code_rows, width), F32),
            *[pltpu.VMEM((2 * seq_count, count, 128), F32) for count in lines],
            landings,
            dma((11,)),
            dma((4,)),
            dma((4,)),
            dma((4,)),
            dma((4,)),
            dma((width // ITER,)),
            dma((width // ITER,)),
            dma((smalls,)),
            dma((smalls,)),
            dma((sem_count,)),
            dma((sem_count,)),
        ],
        compiler_params=pltpu.CompilerParams(
            collective_id=0, has_side_effects=True, vmem_limit_bytes=VMEM_BYTES
        ),
    )(
        inputs,
        cotangent,
        cond_mask,
        timestep,
        embed_table,
        cond_bias.reshape(6 * width // 128, 128),
        jnp.asarray(cosine),
        jnp.asarray(sine),
        mix_weight,
        project_weight,
        up_weight,
        down_weight,
        cond_weight,
    )
    return finish(layer, igrad, share_mix, share_project, share_up, share_down, gall, batch_count)


def finish_kernel(
    batch_count,
    layer_in,
    igrad_in,
    mix_in,
    project_in,
    up_in,
    down_in,
    early_in,
    late_in,
    layer,
    igrad,
    mix,
    project,
    up,
    down,
    cond,
    bias,
    igrad16,
    igrad32,
    early,
    late,
    cond_here,
    layer16,
    project_here,
    up_here,
    down_here,
    mix_here,
    project32,
    up32,
    down32,
    mix32,
    sem,
):
    width = igrad.shape[-1]
    copies = [
        pltpu.make_async_copy(early_in, early, sem.at[sem.shape[0] - 1]),
        pltpu.make_async_copy(late_in, late, sem.at[0]),
    ]
    parts = igrad16.shape[0]
    height = igrad16.shape[1]
    view = [divmod(n * height, igrad.shape[1]) for n in range(parts)]
    loads = [
        pltpu.make_async_copy(
            igrad_in.at[j, pl.ds(row, height), :], igrad16.at[n], sem.at[1 + n]
        )
        for n, (j, row) in enumerate(view)
    ]
    for copy in copies + loads:
        copy.start()
    k = 1 + parts
    moves = [
        (layer_in, layer16, layer16, layer),
        (project_in, project_here, project32, project),
        (up_in, up_here, up32, up),
        (down_in, down_here, down32, down),
        (mix_in, mix_here, mix32, mix),
    ]
    moves_in = [
        pltpu.make_async_copy(source, here, sem.at[k + n])
        for n, (source, here, _, _) in enumerate(moves)
    ]
    for copy in moves_in:
        copy.start()
    k += len(moves)
    outs = []
    for n, (j, row) in enumerate(view):
        loads[n].wait()
        igrad32[n] = igrad16[n].astype(F32)
        outs.append(
            pltpu.make_async_copy(
                igrad32.at[n], igrad.at[j, pl.ds(row, height), :], sem.at[k + n]
            )
        )
        outs[-1].start()
    k += parts
    for n, (_, narrow, here, target) in enumerate(moves):
        moves_in[n].wait()
        if n > 0:
            here[...] = narrow[...].astype(F32)
        pieces = [(here, target)]
        if n == len(moves) - 1:
            pieces = [
                (
                    here.at[:, pl.ds((3 * i + part) * ITER, ITER)],
                    target.at[:, pl.ds(part * width + i * ITER, ITER)],
                )
                for i in range(width // ITER)
                for part in range(3)
            ]
        for here, target in pieces:
            outs.append(pltpu.make_async_copy(here, target, sem.at[k]))
            outs[-1].start()
            k += 1
    for copy in copies:
        copy.wait()
    b = lax.axis_index("batch")
    strips = width // 128
    codes = jnp.concatenate([early[:, n, :] for n in range(4 * strips, 5 * strips)], axis=1)
    grads = jnp.concatenate(
        [late[:, n, :] for n in range(2 * strips)] + [early[:, n, :] for n in range(4 * strips)],
        axis=1,
    )
    mine = width // batch_count
    codes = pltpu.roll(codes, lax.rem(width - b * mine, width), 1)[:, :mine]
    cond_here[...] = lax.dot_general(
        codes,
        grads,
        (((0,), (0,)), ((), ())),
        precision=lax.Precision.HIGHEST,
        preferred_element_type=F32,
    )
    outs.append(pltpu.make_async_copy(cond_here, cond, sem.at[k]))
    outs[-1].start()
    mine = 6 * width // batch_count
    total = jnp.broadcast_to(col_sum(grads), (8, 6 * width))
    total = pltpu.roll(total, lax.rem(6 * width - b * mine, 6 * width), 1)
    bias[...] = total[0, :mine]
    for copy in outs:
        copy.wait()


def finish(layer, igrad, mix, project, up, down, gall, batch_count):
    width = layer.shape[-1]
    vmem = pl.BlockSpec(memory_space=pltpu.VMEM)
    hbm = pl.BlockSpec(memory_space=pl.ANY)
    rows = layer.shape[0] * layer.shape[1]
    parts = 4
    shape = jax.ShapeDtypeStruct
    outs = pl.pallas_call(
        functools.partial(finish_kernel, batch_count),
        name="finish",
        out_shape=[
            shape(layer.shape, BF),
            shape(igrad.shape, F32),
            shape(mix.shape, F32),
            shape(project.shape, F32),
            shape(up.shape, F32),
            shape(down.shape, F32),
            shape((width // batch_count, 6 * width), F32),
            shape((6 * width // batch_count,), F32),
        ],
        in_specs=[hbm] * 8,
        out_specs=[hbm] * 7 + [vmem],
        scratch_shapes=[
            pltpu.VMEM((parts, rows // parts, width), BF),
            pltpu.VMEM((parts, rows // parts, width), F32),
            *[pltpu.VMEM(part.shape, F32) for part in gall],
            pltpu.VMEM((width // batch_count, 6 * width), F32),
            pltpu.VMEM(layer.shape, BF),
            *[pltpu.VMEM(share.shape, BF) for share in (project, up, down, mix)],
            *[pltpu.VMEM(share.shape, F32) for share in (project, up, down, mix)],
            pltpu.SemaphoreType.DMA((12 + 2 * parts + 3 * (width // ITER),)),
        ],
        compiler_params=pltpu.CompilerParams(vmem_limit_bytes=VMEM_BYTES),
    )(layer, igrad, mix, project, up, down, *gall)
    return tuple(outs)


VMEM_BYTES = 64 * 1024 * 1024 - 512 * 1024


def solution(mesh):
    sizes = (mesh.shape["seq"], mesh.shape["batch"])
    split = P("batch", "seq", None)
    placed = (split, split, P("batch"), P("batch")) + (P(),) * 7
    return jax.shard_map(
        functools.partial(per_device, sizes),
        mesh=mesh,
        in_specs=placed,
        out_specs=(split, split) + (P("batch", None),) * 5 + (P("batch"),),
        check_vma=False,
    )
```
